512 devices in a mesh: dp: 16 (over y, x), seq: 32 (over z, core).
Axes of the slice: x: 4, y: 4, z: 16, core: 2. Of those that a mesh axis runs over, the one named last changes fastest.
Arguments:
- q_in: bfloat16 [65536, 2560], P(('dp', 'seq')), may hold values from -6 to 6
- k_in: bfloat16 [65536, 2560], P(('dp', 'seq')), may hold values from -6 to 6
- v_in: bfloat16 [65536, 2560], P(('dp', 'seq')), may hold values from -6 to 6
- gain_q: float32 [2560], replicated, may hold values from 0.5 to 1.5
- gain_k: float32 [2560], replicated, may hold values from 0.5 to 1.5
- d_out: bfloat16 [65536, 2560], P(('dp', 'seq')), may hold values from -6 to 6
- video: int32 [512], P(('dp', 'seq')), may hold values from 0 to 127, never falling along the last dimension, each value on 1 to 8 neighbouring positions
Outputs:
- dq_in: bfloat16 [65536, 2560], P(('dp', 'seq'))
- dk_in: bfloat16 [65536, 2560], P(('dp', 'seq'))
- dv_in: bfloat16 [65536, 2560], P(('dp', 'seq'))
- dgain_q: float32 [2560], replicated
- dgain_k: float32 [2560], replicated
The draws below stay inside these ranges and needn't reach their ends.
Inputs may be any that keep to these rules, and one draw needn't show every extreme that they name: Video ids never fall along the group order; each video holds 1 to 8 consecutive groups and one holds exactly 8.
All inputs are finite; a program needn't handle non-finite values.
Results may differ from the reference program's by a relative error of at most 0.0079.
Values may be sent and summed in bfloat16 or wider, within the bound.
No kernel may reach another device: no remote copies, remote signals or barrier semaphores. Data moves between devices by JAX's collectives and lax.ppermute only.
A program may use at most 128 MiB of HBM per device.

```python
import math
import jax
import jax.numpy as jnp
import numpy as np
from jax import lax

HEADS = 20
HSIZE = 128
GROUP = 128
WIN = 4
VMAX = 8
VIDEOS = 128
TOKENS = 65536
DEVICES = 512


def draw_q_in(key, part):
    own_key = jax.random.fold_in(key, 11)
    width = HEADS * HSIZE
    values = jnp.clip(jax.random.normal(own_key, (TOKENS, width), jnp.float32), -6.0, 6.0)
    return values.astype(jnp.bfloat16)


def draw_k_in(key, part):
    own_key = jax.random.fold_in(key, 12)
    width = HEADS * HSIZE
    values = jnp.clip(jax.random.normal(own_key, (TOKENS, width), jnp.float32), -6.0, 6.0)
    return values.astype(jnp.bfloat16)


def level_of(key, shape, cuts, least, high):
    level, own = 1.0, jax.random.fold_in(key, 6)
    for dim, parts in cuts:
        draws = jnp.exp(jax.random.uniform(jax.random.fold_in(own, dim), (parts,), jnp.float32, least / len(cuts), high / len(cuts)))
        level = level * jnp.repeat(draws, shape[dim] // parts).reshape([-1 if axis == dim else 1 for axis in range(len(shape))])
    return level


def split_up(count, total, reach, skew):
    loads = [(1 << 20) // math.isqrt(grade ** skew) + 1 for grade in range(2, count + 1)]
    spare, counts = total - reach - (count - 1), [1] * (count - 1)
    while spare > 0:
        free = [i for i in range(count - 1) if counts[i] < reach]
        mass, budget = sum([loads[i] for i in free]), spare
        for i in free:
            addition = min(reach - counts[i], max(1, budget * loads[i] // mass), spare)
            counts[i] = counts[i] + addition
            spare = spare - addition
    return np.array([reach] + counts)


def uneven(key, amount, total, most, slope):
    if amount == 2:
        one = jax.random.randint(key, (), max(1, total - most), min(most, total - 1) + 1)
        return jnp.stack([one, total - one])
    tallies = jnp.asarray(split_up(amount, total, most, slope), jnp.int32)
    couples = (amount - 1) // 2
    donor, sink = tallies[1:1 + 2 * couples:2], tallies[2:2 + 2 * couples:2]
    slack = jnp.minimum(donor - 1, most - sink)
    shifted = jax.random.randint(jax.random.fold_in(key, 1), (couples,), 0, 1 << 20) % (slack + 1)
    tallies = tallies.at[1:1 + 2 * couples:2].set(donor - shifted).at[2:2 + 2 * couples:2].set(sink + shifted)
    return tallies[jax.random.permutation(jax.random.fold_in(key, 2), amount)]


def noise(stream_key, extent, scale, reach, shards=(), kind=jnp.bfloat16):
    level = level_of(stream_key, extent, shards, -0.22, 0.18) if shards else 1.0
    entries = jax.random.normal(stream_key, extent, jnp.float32) * scale * level
    return jnp.minimum(jnp.maximum(entries, -reach), reach).astype(kind)


def setup_inputs(seed: int = 0) -> dict:
    key_of = jax.random.split(jax.random.key(seed), 8)
    return {
        "q_in": draw_q_in(jax.random.fold_in(key_of[7], 71), 0),
        "k_in": draw_k_in(jax.random.fold_in(key_of[7], 71), 0),
        "v_in": noise(key_of[2], (TOKENS, HEADS * HSIZE), 1.0, 6.0, ((0, 512),)),
        "gain_q": jnp.clip(1.0 + 0.1 * jax.random.normal(key_of[3], (HEADS * HSIZE,), jnp.float32), 0.5, 1.5),
        "gain_k": jnp.clip(1.0 + 0.1 * jax.random.normal(key_of[4], (HEADS * HSIZE,), jnp.float32), 0.5, 1.5),
        "d_out": noise(key_of[5], (TOKENS, HEADS * HSIZE), 1.0, 6.0, ((0, 512),)),
        "video": jnp.searchsorted(jnp.cumsum(uneven(key_of[6], VIDEOS, DEVICES, VMAX, 0)), jnp.arange(DEVICES), side="right").astype(jnp.int32),
    }


EPS = 1e-06
NEG = -1e+30

def normed(values, gain):
    values = values.astype(jnp.float32)
    factor = lax.rsqrt(lax.optimization_barrier(jnp.mean(values * values, axis=-1, keepdims=True)) + EPS)
    return values * factor * gain

def reference(q_in, k_in, v_in, gain_q, gain_k, d_out, video):
    feat_width = HEADS * HSIZE
    score_scale = 1.0 / math.sqrt(HSIZE)
    q_norm = normed(q_in, gain_q).astype(jnp.bfloat16)
    k_norm = normed(k_in, gain_k).astype(jnp.bfloat16)
    q_blocks = q_norm.reshape(DEVICES, GROUP, HEADS, HSIZE)
    k_blocks = k_norm.reshape(DEVICES, GROUP, HEADS, HSIZE)
    v_blocks = v_in.reshape(DEVICES, GROUP, HEADS, HSIZE)
    d_blocks = d_out.reshape(DEVICES, GROUP, HEADS, HSIZE)
    q_raw = q_in.reshape(DEVICES, GROUP, feat_width)
    k_raw = k_in.reshape(DEVICES, GROUP, feat_width)
    marker = (video + 1).astype(jnp.int32)
    padding = WIN - 1
    blank = jnp.zeros((padding, GROUP, HEADS, HSIZE), jnp.bfloat16)
    blank_mark = jnp.zeros((padding,), jnp.int32)
    k_front = jnp.concatenate([blank, k_blocks], 0)
    v_front = jnp.concatenate([blank, v_blocks], 0)
    mark_front = jnp.concatenate([blank_mark, marker], 0)

    def query_pass(index):
        own_q = lax.dynamic_index_in_dim(q_blocks, index, 0, False)
        own_d = lax.dynamic_index_in_dim(d_blocks, index, 0, False)
        keys_win = lax.dynamic_slice_in_dim(k_front, index, WIN, 0).reshape(WIN * GROUP, HEADS, HSIZE)
        vals_win = lax.dynamic_slice_in_dim(v_front, index, WIN, 0).reshape(WIN * GROUP, HEADS, HSIZE)
        marks_win = lax.dynamic_slice_in_dim(mark_front, index, WIN, 0)
        own_mark = lax.dynamic_index_in_dim(marker, index, 0, False)
        key_ok = jnp.repeat(marks_win == own_mark, GROUP)
        scores = jnp.einsum('qhd,khd->hqk', own_q.astype(jnp.float32), keys_win.astype(jnp.float32)) * score_scale
        masked = jnp.where(key_ok[None, None, :], scores, NEG)
        row_max = lax.optimization_barrier(jnp.max(masked, axis=-1))
        log_total = row_max + jnp.log(lax.optimization_barrier(jnp.sum(jnp.exp(masked - row_max[..., None]), axis=-1)))
        prob = jnp.exp(masked - log_total[..., None])
        prob_bf = prob.astype(jnp.bfloat16)
        attn_out = jnp.einsum('hqk,khd->qhd', prob_bf.astype(jnp.float32), vals_win.astype(jnp.float32))
        delta = jnp.transpose(lax.optimization_barrier(jnp.sum(own_d.astype(jnp.float32) * attn_out, axis=-1)))
        dprob = jnp.einsum('qhd,khd->hqk', own_d.astype(jnp.float32), vals_win.astype(jnp.float32))
        dscore = prob * (dprob - delta[..., None])
        dscore_bf = (dscore * score_scale).astype(jnp.bfloat16)
        dq_norm = jnp.einsum('hqk,khd->qhd', dscore_bf.astype(jnp.float32), keys_win.astype(jnp.float32))
        raw_block = lax.dynamic_index_in_dim(q_raw, index, 0, False).astype(jnp.float32)
        _, pull_back = jax.vjp(normed, raw_block, gain_q)
        dq_block, dgain_part = pull_back(dq_norm.reshape(GROUP, feat_width))
        return (dq_block.astype(jnp.bfloat16), log_total, delta, dgain_part)
    indices = jnp.arange(DEVICES, dtype=jnp.int32)
    dq_all, lse_all, delta_all, dgain_q_parts = lax.map(query_pass, indices)
    q_back = jnp.concatenate([q_blocks, blank], 0)
    d_back = jnp.concatenate([d_blocks, blank], 0)
    stat_blank = jnp.zeros((padding, HEADS, GROUP), jnp.float32)
    lse_back = jnp.concatenate([lse_all, stat_blank], 0)
    delta_back = jnp.concatenate([delta_all, stat_blank], 0)
    mark_back = jnp.concatenate([marker, blank_mark], 0)

    def key_pass(index):
        own_k = lax.dynamic_index_in_dim(k_blocks, index, 0, False)
        own_v = lax.dynamic_index_in_dim(v_blocks, index, 0, False)
        q_win = lax.dynamic_slice_in_dim(q_back, index, WIN, 0).reshape(WIN * GROUP, HEADS, HSIZE)
        d_win = lax.dynamic_slice_in_dim(d_back, index, WIN, 0).reshape(WIN * GROUP, HEADS, HSIZE)
        lse_win = jnp.transpose(lax.dynamic_slice_in_dim(lse_back, index, WIN, 0), (1, 0, 2)).reshape(HEADS, WIN * GROUP)
        delta_win = jnp.transpose(lax.dynamic_slice_in_dim(delta_back, index, WIN, 0), (1, 0, 2)).reshape(HEADS, WIN * GROUP)
        marks_win = lax.dynamic_slice_in_dim(mark_back, index, WIN, 0)
        own_mark = lax.dynamic_index_in_dim(marker, index, 0, False)
        query_ok = jnp.repeat(marks_win == own_mark, GROUP)
        scores = jnp.einsum('qhd,khd->hqk', q_win.astype(jnp.float32), own_k.astype(jnp.float32)) * score_scale
        prob = jnp.where(query_ok[None, :, None], jnp.exp(scores - lse_win[..., None]), 0.0)
        prob_bf = prob.astype(jnp.bfloat16)
        dprob = jnp.einsum('qhd,khd->hqk', d_win.astype(jnp.float32), own_v.astype(jnp.float32))
        dscore = prob * (dprob - delta_win[..., None])
        dscore_bf = (dscore * score_scale).astype(jnp.bfloat16)
        q_parts = q_win.reshape(WIN, GROUP, HEADS, HSIZE).astype(jnp.float32)
        d_parts = d_win.reshape(WIN, GROUP, HEADS, HSIZE).astype(jnp.float32)
        dk_parts = jnp.einsum('hwqk,wqhd->wkhd', dscore_bf.reshape(HEADS, WIN, GROUP, GROUP).astype(jnp.float32), q_parts).astype(jnp.bfloat16)
        dv_parts = jnp.einsum('hwqk,wqhd->wkhd', prob_bf.reshape(HEADS, WIN, GROUP, GROUP).astype(jnp.float32), d_parts).astype(jnp.bfloat16)
        dk_parts, dv_parts = lax.optimization_barrier((dk_parts, dv_parts))
        dk_norm = lax.optimization_barrier(jnp.sum(dk_parts.astype(jnp.float32), axis=0))
        dv_block = lax.optimization_barrier(jnp.sum(dv_parts.astype(jnp.float32), axis=0))
        raw_block = lax.dynamic_index_in_dim(k_raw, index, 0, False).astype(jnp.float32)
        _, pull_back = jax.vjp(normed, raw_block, gain_k)
        dk_block, dgain_part = pull_back(dk_norm.reshape(GROUP, feat_width))
        return (dk_block.astype(jnp.bfloat16), dv_block.reshape(GROUP, feat_width).astype(jnp.bfloat16), dgain_part)
    dk_all, dv_all, dgain_k_parts = lax.map(key_pass, indices)
    dq_in = dq_all.reshape(DEVICES * GROUP, feat_width)
    dk_in = dk_all.reshape(DEVICES * GROUP, feat_width)
    dv_in = dv_all.reshape(DEVICES * GROUP, feat_width)
    return (dq_in, dk_in, dv_in, lax.optimization_barrier(jnp.sum(dgain_q_parts, axis=0)), lax.optimization_barrier(jnp.sum(dgain_k_parts, axis=0)))
```

```python
import functools
import math

import jax
import jax.numpy as jnp
from jax import lax
from jax.experimental import pallas as pl
from jax.experimental.pallas import tpu as pltpu
from jax.sharding import PartitionSpec as P

HSIZE = 128
WIN = 4
EPS = 1e-06
NEG = -1e30
MARK_ROWS = 16
AXES = ("dp", "seq")
VMEM_LIMIT = 40 * 1024 * 1024
F32 = jnp.float32
BF16 = jnp.bfloat16


def dot_nt(a, b):
    return lax.dot_general(a, b, (((1,), (1,)), ((), ())), preferred_element_type=F32)


def dot_nn(a, b):
    return lax.dot_general(a, b, (((1,), (0,)), ((), ())), preferred_element_type=F32)


def pack_kernel(heads, odd_ref, video_ref, q_ref, k_ref, v_ref, d_ref, gq_ref, gk_ref, a_ref, b_ref, rq_ref, rk_ref):
    odd = odd_ref[0] == 1
    rows = q_ref.shape[0]
    width = q_ref.shape[1]
    q_raw = q_ref[...].astype(F32)
    k_raw = k_ref[...].astype(F32)
    rq = lax.rsqrt(jnp.sum(q_raw * q_raw, axis=-1, keepdims=True) * (1.0 / width) + EPS)
    rk = lax.rsqrt(jnp.sum(k_raw * k_raw, axis=-1, keepdims=True) * (1.0 / width) + EPS)
    rq_ref[...] = jnp.broadcast_to(rq, rq_ref.shape)
    rk_ref[...] = jnp.broadcast_to(rk, rk_ref.shape)
    for h in range(heads):
        cols = slice(h * HSIZE, (h + 1) * HSIZE)
        qn = (q_ref[:, cols].astype(F32) * rq * gq_ref[:, cols]).astype(BF16)
        kn = (k_ref[:, cols].astype(F32) * rk * gk_ref[:, cols]).astype(BF16)
        v = v_ref[:, cols]
        d = d_ref[:, cols]
        top = slice(2 * h * rows, (2 * h + 1) * rows)
        low = slice((2 * h + 1) * rows, (2 * h + 2) * rows)
        a_ref[top, :] = jnp.where(odd, kn, qn)
        b_ref[top, :] = jnp.where(odd, qn, kn)
        a_ref[low, :] = jnp.where(odd, v, d)
        b_ref[low, :] = jnp.where(odd, d, v)
    mark = jnp.full((MARK_ROWS, HSIZE), (video_ref[0] + 1).astype(F32), F32).astype(BF16)
    a_ref[2 * heads * rows :, :] = mark
    b_ref[2 * heads * rows :, :] = mark


def bias_of(odd, own_mark, x_mark, s_mark, take_s):
    mark = jnp.where(odd == take_s, s_mark[0:1, 0:1].astype(F32), x_mark[0:1, 0:1].astype(F32))
    return jnp.where(mark == own_mark, 0.0, NEG)


def query_kernel(heads, per, factor, odd_ref, a, b, x1, s1, x2, s2, x3, s3, am, x1m, s1m, x2m, s2m, x3m, s3m,
                 q_ref, gq_ref, rq_ref, t_ref, w_ref, u_ref, stat_ref, stat_acc):
    step = pl.program_id(0)
    odd = odd_ref[0] == 1
    rows = q_ref.shape[0]
    own_mark = am[0:1, 0:1].astype(F32)
    biases = [bias_of(odd, own_mark, xm, sm, True) for xm, sm in ((x1m, s1m), (x2m, s2m), (x3m, s3m))]
    lane = lax.broadcasted_iota(jnp.int32, (rows, HSIZE), 1)
    scale = 1.0 / math.sqrt(HSIZE)

    @pl.when(step == 0)
    def _():
        u_ref[...] = jnp.zeros_like(u_ref)
        stat_acc[...] = jnp.zeros_like(stat_acc)

    for j in range(per):
        top = slice(2 * j * rows, (2 * j + 1) * rows)
        low = slice((2 * j + 1) * rows, (2 * j + 2) * rows)
        cols = slice(j * HSIZE, (j + 1) * HSIZE)
        q = jnp.where(odd, b[top, :], a[top, :])
        d_out = jnp.where(odd, b[low, :], a[low, :])
        keys = [jnp.where(odd, a[top, :], b[top, :])] + [
            jnp.where(odd, s[top, :], x[top, :]) for x, s in ((x1, s1), (x2, s2), (x3, s3))
        ]
        vals = [jnp.where(odd, a[low, :], b[low, :])] + [
            jnp.where(odd, s[low, :], x[low, :]) for x, s in ((x1, s1), (x2, s2), (x3, s3))
        ]
        scores = [dot_nt(q, key) for key in keys]
        dprobs = [dot_nt(d_out, val) for val in vals]
        top_of = jnp.max(scores[0], axis=-1, keepdims=True) * factor
        for score, bias in zip(scores[1:], biases):
            top_of = jnp.maximum(top_of, jnp.max(score, axis=-1, keepdims=True) * factor + bias)
        probs = [jnp.exp2(scores[0] * factor - top_of)] + [
            jnp.exp2(score * factor + (bias - top_of)) for score, bias in zip(scores[1:], biases)
        ]
        total = jnp.sum(probs[0] + probs[1] + probs[2] + probs[3], axis=-1, keepdims=True)
        mixed = jnp.sum(
            probs[0] * dprobs[0] + probs[1] * dprobs[1] + probs[2] * dprobs[2] + probs[3] * dprobs[3],
            axis=-1, keepdims=True,
        )
        inverse = 1.0 / total
        delta = mixed * inverse
        dq = None
        for prob, dprob, key in zip(probs, dprobs, keys):
            term = dot_nn(((prob * inverse) * (dprob - delta)).astype(BF16), key)
            dq = term if dq is None else dq + term
        dq = dq * scale
        raw = q_ref[:, cols].astype(F32)
        tilted = dq * gq_ref[:, cols]
        t_ref[:, cols] = tilted
        u_ref[...] += jnp.sum(raw * tilted, axis=-1, keepdims=True)
        w_ref[0, j : j + 1, :] = jnp.sum(dq * (raw * rq_ref[...]), axis=0, keepdims=True)
        head = step * per + j
        log_total = top_of + jnp.log2(total)
        stat_acc[...] = jnp.where(
            lane == head, log_total, jnp.where(lane == head + heads, delta, stat_acc[...])
        )

    @pl.when(step == heads // per - 1)
    def _():
        stat_ref[...] = jnp.transpose(stat_acc[...])[: 2 * heads, :]


def key_kernel(heads, per, factor, odd_ref, a, b, x1, s1, x2, s2, x3, s3, am, x1m, s1m, x2m, s2m, x3m, s3m,
               t0_ref, t1_ref, t2_ref, t3_ref, k_ref, gk_ref, rk_ref, dk_ref, dv_ref, tilt, u_acc):
    step = pl.program_id(0)
    odd = odd_ref[0] == 1
    rows = k_ref.shape[0]
    width = k_ref.shape[1]
    own_mark = am[0:1, 0:1].astype(F32)
    biases = [jnp.zeros((1, 1), F32)] + [
        bias_of(odd, own_mark, xm, sm, False) for xm, sm in ((x1m, s1m), (x2m, s2m), (x3m, s3m))
    ]
    scale = 1.0 / math.sqrt(HSIZE)

    @pl.when(step == 0)
    def _():
        u_acc[...] = jnp.zeros_like(u_acc)

    for j in range(per):
        top = slice(2 * j * rows, (2 * j + 1) * rows)
        low = slice((2 * j + 1) * rows, (2 * j + 2) * rows)
        head = step * per + j
        key = jnp.where(odd, a[top, :], b[top, :])
        val = jnp.where(odd, a[low, :], b[low, :])
        queries = [jnp.where(odd, b[top, :], a[top, :])] + [
            jnp.where(odd, x[top, :], s[top, :]) for x, s in ((x1, s1), (x2, s2), (x3, s3))
        ]
        d_outs = [jnp.where(odd, b[low, :], a[low, :])] + [
            jnp.where(odd, x[low, :], s[low, :]) for x, s in ((x1, s1), (x2, s2), (x3, s3))
        ]
        dk = None
        dv = None
        for query, d_out, stat, bias in zip(queries, d_outs, (t0_ref, t1_ref, t2_ref, t3_ref), biases):
            log_total = stat[pl.ds(head, 1), :]
            delta = stat[pl.ds(head + heads, 1), :]
            prob = jnp.exp2(dot_nt(key, query) * factor + (bias - log_total))
            dscore = prob * (dot_nt(val, d_out) - delta)
            dv_term = dot_nn(prob.astype(BF16), d_out)
            dk_term = dot_nn(dscore.astype(BF16), query)
            dv = dv_term if dv is None else dv + dv_term
            dk = dk_term if dk is None else dk + dk_term
        dv_ref[:, j * HSIZE : (j + 1) * HSIZE] = dv.astype(BF16)
        cols = pl.ds(pl.multiple_of(head * HSIZE, HSIZE), HSIZE)
        tilted = dk * scale * gk_ref[:, cols]
        tilt[:, cols] = tilted
        u_acc[...] += jnp.sum(k_ref[:, cols].astype(F32) * tilted, axis=-1, keepdims=True)

    @pl.when(step == heads // per - 1)
    def _():
        rk = rk_ref[...]
        low_part = rk * rk * rk * u_acc[...] * (1.0 / width)
        for h in range(heads):
            cols = slice(h * HSIZE, (h + 1) * HSIZE)
            dk_ref[:, cols] = (rk * tilt[:, cols] - k_ref[:, cols].astype(F32) * low_part).astype(BF16)


def close_kernel(heads, q_ref, t_ref, u_ref, rq_ref, dq_ref):
    rq = rq_ref[...]
    low_part = rq * rq * rq * u_ref[...] * (1.0 / q_ref.shape[1])
    for h in range(heads):
        cols = slice(h * HSIZE, (h + 1) * HSIZE)
        dq_ref[:, cols] = (rq * t_ref[:, cols] - q_ref[:, cols].astype(F32) * low_part).astype(BF16)


def smem():
    return pl.BlockSpec(memory_space=pltpu.SMEM)


def vmem():
    return pl.BlockSpec(memory_space=pltpu.VMEM)


def body(q_in, k_in, v_in, gain_q, gain_k, d_out, video):
    rows, width = q_in.shape
    heads = width // HSIZE
    per = 4
    steps = heads // per
    factor = math.log2(math.e) / math.sqrt(HSIZE)
    groups = lax.axis_size("dp") * lax.axis_size("seq")
    odd = (lax.axis_index("seq") % 2).astype(jnp.int32).reshape(1)
    gq = gain_q.reshape(1, width)
    gk = gain_k.reshape(1, width)
    params = pltpu.CompilerParams(vmem_limit_bytes=VMEM_LIMIT, dimension_semantics=("arbitrary",))
    packed = jax.ShapeDtypeStruct((2 * heads * rows + MARK_ROWS, HSIZE), BF16)
    wide = jax.ShapeDtypeStruct((rows, HSIZE), F32)
    a, b, rq, rk = pl.pallas_call(
        functools.partial(pack_kernel, heads),
        out_shape=(packed, packed, wide, wide),
        in_specs=[smem(), smem()] + [vmem()] * 6,
        out_specs=[vmem()] * 4,
        compiler_params=pltpu.CompilerParams(vmem_limit_bytes=VMEM_LIMIT),
        name="pack",
    )(odd, video, q_in, k_in, v_in, d_out, gq, gk)

    cross = [(i, i + 1) for i in range(1, groups - 1, 2)] + [(i, i - 1) for i in range(2, groups, 2)]
    chip = [(i, i ^ 1) for i in range(groups)]

    def over(value):
        return lax.ppermute(value, AXES, cross)

    def within(value):
        return lax.ppermute(value, AXES, chip)

    x1 = over(a)
    s1 = within(b)
    x2 = over(s1)
    s2 = within(x1)
    x3 = over(s2)
    s3 = within(x2)
    blocks = (a, b, x1, s1, x2, s2, x3, s3)
    marks = (a, x1, s1, x2, s2, x3, s3)
    block_spec = pl.BlockSpec((2 * per * rows, HSIZE), lambda i: (i, 0))
    mark_spec = pl.BlockSpec((MARK_ROWS, HSIZE), lambda i: (2 * heads * rows // MARK_ROWS, 0))
    col_spec = pl.BlockSpec((rows, per * HSIZE), lambda i: (0, i))
    gain_spec = pl.BlockSpec((1, per * HSIZE), lambda i: (0, i))
    still = lambda shape: pl.BlockSpec(shape, lambda i: (0, 0))
    pair_flops = 2 * rows * rows * HSIZE * heads
    stats_shape = (2 * heads, rows)
    tilted, w, u, stats = pl.pallas_call(
        functools.partial(query_kernel, heads, per, factor),
        grid=(steps,),
        out_shape=(
            jax.ShapeDtypeStruct((rows, width), F32),
            jax.ShapeDtypeStruct((steps, per, HSIZE), F32),
            wide,
            jax.ShapeDtypeStruct(stats_shape, F32),
        ),
        in_specs=[smem()] + [block_spec] * 8 + [mark_spec] * 7 + [col_spec, gain_spec, still((rows, HSIZE))],
        out_specs=[
            col_spec,
            pl.BlockSpec((1, per, HSIZE), lambda i: (i, 0, 0)),
            still((rows, HSIZE)),
            still(stats_shape),
        ],
        scratch_shapes=[pltpu.VMEM((rows, HSIZE), F32)],
        compiler_params=params,
        cost_estimate=pl.CostEstimate(flops=12 * pair_flops, bytes_accessed=8 * 2**20, transcendentals=0),
        name="query_side",
    )(odd, *blocks, *marks, q_in, gq, rq)

    dp, seq = lax.axis_size("dp"), lax.axis_size("seq")
    w = w.reshape(heads, HSIZE)
    w = lax.all_to_all(jnp.broadcast_to(w[None], (dp, heads, HSIZE)), "dp", 0, 0)
    w = jnp.sum(w, axis=0).astype(BF16)
    w = lax.all_to_all(jnp.broadcast_to(w[None], (seq, heads, HSIZE)), "seq", 0, 0)
    dgain_q = jnp.sum(w.astype(F32), axis=0).reshape(width)
    dgain_k = dgain_q * gain_q / gain_k

    from_one = lax.ppermute(stats, AXES, [(i, i - 1) for i in range(1, groups)])
    from_two = lax.ppermute(stats, AXES, [(i, i - 2) for i in range(2, groups)])
    from_three = lax.ppermute(stats, AXES, [(i, i - 3) for i in range(3, groups)])

    dk_in, dv_in = pl.pallas_call(
        functools.partial(key_kernel, heads, per, factor),
        grid=(steps,),
        out_shape=(
            jax.ShapeDtypeStruct((rows, width), BF16),
            jax.ShapeDtypeStruct((rows, width), BF16),
        ),
        in_specs=[smem()] + [block_spec] * 8 + [mark_spec] * 7 + [still(stats_shape)] * 4
        + [still((rows, width)), still((1, width)), still((rows, HSIZE))],
        out_specs=[still((rows, width)), col_spec],
        scratch_shapes=[pltpu.VMEM((rows, width), F32), pltpu.VMEM((rows, HSIZE), F32)],
        compiler_params=params,
        cost_estimate=pl.CostEstimate(flops=16 * pair_flops, bytes_accessed=8 * 2**20, transcendentals=0),
        name="key_side",
    )(odd, *blocks, *marks, stats, from_one, from_two, from_three, k_in, gk, rk)

    dq_in = pl.pallas_call(
        functools.partial(close_kernel, heads),
        out_shape=jax.ShapeDtypeStruct((rows, width), BF16),
        in_specs=[vmem()] * 4,
        out_specs=vmem(),
        compiler_params=pltpu.CompilerParams(vmem_limit_bytes=VMEM_LIMIT),
        name="close_q",
    )(q_in, tilted, u, rq)
    return dq_in, dk_in, dv_in, dgain_q, dgain_k


def solution(mesh):
    rows = P(("dp", "seq"), None)
    return jax.shard_map(
        body,
        mesh=mesh,
        in_specs=(rows, rows, rows, P(), P(), rows, P(("dp", "seq"))),
        out_specs=(rows, rows, rows, P(), P()),
        check_vma=False,
    )
```

```python
import functools
import math

import jax
import jax.numpy as jnp
from jax import lax
from jax.experimental import pallas as pl
from jax.experimental.pallas import tpu as pltpu
from jax.sharding import Mesh
from jax.sharding import PartitionSpec as P

HSIZE = 128
WIN = 4
EPS = 1e-06
NEG = -1e30
MARK_ROWS = 16
PER = 5
SPLIT = 4
AXES = ("dp", "z", "core")
CORES = 2
VMEM_LIMIT = 63 * 1024 * 1024
F32 = jnp.float32
BF16 = jnp.bfloat16


def dot_nt(a, b):
    return lax.dot_general(a, b, (((1,), (1,)), ((), ())), preferred_element_type=F32)


def dot_nn(a, b):
    return lax.dot_general(a, b, (((1,), (0,)), ((), ())), preferred_element_type=F32)


def head_rows(j, rows):
    return slice(j * rows, (j + 1) * rows)


def head_cols(j):
    return slice(j * HSIZE, (j + 1) * HSIZE)


def pack_kernel(heads, odd_ref, video_ref, q_hbm, k_hbm, d_hbm, v_hbm, gq_hbm, gk_hbm,
                a_hbm, b_hbm, rq_ref, rk_ref, main, stage, gain, mark, in_sems, out_sems):
    odd = odd_ref[0] == 1
    rows, width = q_hbm.shape
    size = rows // SPLIT
    steps = heads // PER
    span = PER * rows

    def load(which, src):
        return [
            pltpu.make_async_copy(
                src.at[pl.ds(part * size, size), :], main.at[which, pl.ds(part * size, size), :], in_sems.at[which, part]
            )
            for part in range(SPLIT)
        ]

    loads = [load(which, src) for which, src in enumerate((q_hbm, k_hbm, d_hbm, v_hbm))]
    gains = [
        pltpu.make_async_copy(src, gain.at[which], in_sems.at[which, SPLIT]) for which, src in enumerate((gq_hbm, gk_hbm))
    ]
    for copy in gains + loads[0] + loads[1] + loads[2] + loads[3]:
        copy.start()

    def store(which, step, dst):
        if step == steps:
            return pltpu.make_async_copy(
                mark, dst.at[pl.ds(2 * steps * span, MARK_ROWS), :], out_sems.at[which, steps]
            )
        return pltpu.make_async_copy(
            stage.at[which, pl.ds(step * span, span), :],
            dst.at[pl.ds((2 * step + which // 2) * span, span), :],
            out_sems.at[which, step],
        )

    def start_store(which, step):
        with_a = odd == (which % 2 == 1)

        @pl.when(with_a)
        def _():
            store(which, step, a_hbm).start()

        @pl.when(jnp.logical_not(with_a))
        def _():
            store(which, step, b_hbm).start()

    mark[...] = jnp.full((MARK_ROWS, HSIZE), (video_ref[0] + 1).astype(F32), F32).astype(BF16)
    for which in range(2):
        start_store(which, steps)
    for copy in gains:
        copy.wait()
    for which, scale_ref in enumerate((rq_ref, rk_ref)):
        for copy in loads[which]:
            copy.wait()
        raw = main[which].astype(F32)
        scale = lax.rsqrt(jnp.sum(raw * raw, axis=-1, keepdims=True) * (1.0 / width) + EPS)
        scale_ref[...] = jnp.broadcast_to(scale, scale_ref.shape)
        for step in range(steps):
            for h in range(step * PER, (step + 1) * PER):
                normed = main[which, :, head_cols(h)].astype(F32) * scale * gain[which, h : h + 1, :]
                stage[which, head_rows(h, rows), :] = normed.astype(BF16)
            start_store(which, step)
    for which in (2, 3):
        for copy in loads[which]:
            copy.wait()
        for step in range(steps):
            for h in range(step * PER, (step + 1) * PER):
                stage[which, head_rows(h, rows), :] = main[which, :, head_cols(h)]
            start_store(which, step)
    for which in range(4):
        for step in range(steps + (which < 2)):
            store(which, step, a_hbm).wait()


def gate_kernel(*refs):
    del refs


def mark_of(ref):
    return ref[0:1, 0:1].astype(F32)


def bias_of(own_ref, odd, if_odd, if_even):
    mark = jnp.where(odd, mark_of(if_odd), mark_of(if_even))
    return jnp.where(mark == mark_of(own_ref), 0.0, NEG)


def bias_row(biases, rows):
    return jnp.concatenate([jnp.broadcast_to(bias, (1, rows)) for bias in biases], axis=1)


def near_kernel(rows, factor, odd_ref, a, b, x1, s1, x2, s2, am, x1m, s1m, x2m, s2m, g_ref, h_ref, part_ref):
    odd = odd_ref[0] == 1
    bias = bias_row([jnp.zeros((1, 1), F32), bias_of(am, odd, s1m, x1m), bias_of(am, odd, s2m, x2m)], rows)
    pairs = ((a, b), (s1, x1), (s2, x2))
    lane = lax.broadcasted_iota(jnp.int32, (rows, HSIZE), 1)
    keys, scores, dprobs = [], [], []
    for j in range(PER):
        top = head_rows(j, rows)
        low = head_rows(PER + j, rows)
        q = jnp.where(odd, b[top, :], a[top, :])
        d_out = jnp.where(odd, b[low, :], a[low, :])
        keys.append(jnp.concatenate([jnp.where(odd, o[top, :], e[top, :]) for o, e in pairs], axis=0))
        vals = jnp.concatenate([jnp.where(odd, o[low, :], e[low, :]) for o, e in pairs], axis=0)
        scores.append(dot_nt(q, keys[j]))
        dprobs.append(dot_nt(d_out, vals))
    part = jnp.zeros((rows, HSIZE), F32)
    for j in range(PER):
        out = head_rows(j, rows)
        score = scores[j] * factor + bias
        best = jnp.max(score, axis=-1, keepdims=True)
        probs = jnp.exp2(score - best)
        total = jnp.sum(probs, axis=-1, keepdims=True)
        delta = jnp.sum(probs * dprobs[j], axis=-1, keepdims=True) / total
        both = jnp.concatenate([(probs * (dprobs[j] - delta)).astype(BF16), probs.astype(BF16)], axis=0)
        sums = dot_nn(both, keys[j])
        g_ref[out, :] = sums[:rows]
        h_ref[out, :] = sums[rows:]
        for place, value in enumerate((best, total, delta)):
            part = jnp.where(lane == 3 * j + place, value, part)
    part_ref[0] = part


def query_kernel(rows, steps, factor, odd_ref, a, b, x3, s3, am, x3m, s3m, g_ref, h_ref, part_ref,
                 q_ref, gq_ref, rq_ref, dq_ref, w_ref, stat_ref, u_acc, acc_lse, acc_delta, acc_w, tilt):
    step = pl.program_id(0)
    heads = steps * PER
    width = q_ref.shape[1]
    odd = odd_ref[0] == 1
    bias = bias_of(am, odd, s3m, x3m)
    rq = rq_ref[...]
    lane = lax.broadcasted_iota(jnp.int32, (rows, HSIZE), 1)
    scale = 1.0 / math.sqrt(HSIZE)

    @pl.when(step == 0)
    def _():
        u_acc[...] = jnp.zeros_like(u_acc)
        acc_lse[...] = jnp.zeros_like(acc_lse)
        acc_delta[...] = jnp.zeros_like(acc_delta)

    keys, scores, dprobs = [], [], []
    for j in range(PER):
        top = head_rows(j, rows)
        low = head_rows(PER + j, rows)
        q = jnp.where(odd, b[top, :], a[top, :])
        d_out = jnp.where(odd, b[low, :], a[low, :])
        keys.append(jnp.where(odd, s3[top, :], x3[top, :]))
        vals = jnp.where(odd, s3[low, :], x3[low, :])
        scores.append(dot_nt(q, keys[j]))
        dprobs.append(dot_nt(d_out, vals))
    lse = acc_lse[...]
    deltas = acc_delta[...]
    fars, nears = [], []
    for j in range(PER):
        old_best, old_total, old_delta = [
            jnp.sum(jnp.where(lane == 3 * j + place, part_ref[0], 0.0), axis=-1, keepdims=True) for place in range(3)
        ]
        score = scores[j] * factor + bias
        best = jnp.maximum(old_best, jnp.max(score, axis=-1, keepdims=True))
        prob = jnp.exp2(score - best)
        shrink = jnp.exp2(old_best - best)
        old_total = old_total * shrink
        total = old_total + jnp.sum(prob, axis=-1, keepdims=True)
        inverse = 1.0 / total
        delta = (old_total * old_delta + jnp.sum(prob * dprobs[j], axis=-1, keepdims=True)) * inverse
        fars.append(((prob * inverse) * (dprobs[j] - delta)).astype(BF16))
        nears.append((shrink * inverse, old_delta - delta))
        head = step * PER + j
        lse = jnp.where(lane == head, best + jnp.log2(total), lse)
        deltas = jnp.where(lane == head, delta, deltas)
    acc_lse[...] = lse
    acc_delta[...] = deltas
    u_sum = u_acc[...]
    for j in range(PER):
        out = head_rows(j, rows)
        head = step * PER + j
        cols = pl.ds(pl.multiple_of(head * HSIZE, HSIZE), HSIZE)
        part, moved = nears[j]
        dq = (dot_nn(fars[j], keys[j]) + part * (g_ref[out, :] + moved * h_ref[out, :])) * scale
        raw = q_ref[:, cols].astype(F32)
        tilted = dq * gq_ref[pl.ds(head, 1), :]
        tilt[:, cols] = tilted
        u_sum = u_sum + raw * tilted
        acc_w[pl.ds(head, 1), :] = jnp.sum(dq * (raw * rq), axis=0, keepdims=True)
    u_acc[...] = u_sum

    @pl.when(step == steps - 1)
    def _():
        stat_ref[:heads, :] = jnp.transpose(acc_lse[...])[:heads, :]
        stat_ref[heads:, :] = jnp.transpose(acc_delta[...])[:heads, :]
        w_ref[...] = jnp.broadcast_to(acc_w[...].astype(BF16)[None], w_ref.shape)
        low_part = rq * rq * rq * jnp.sum(u_sum, axis=-1, keepdims=True) * (1.0 / width)
        for h in range(heads):
            cols = head_cols(h)
            dq_ref[:, cols] = (rq * tilt[:, cols] - q_ref[:, cols].astype(F32) * low_part).astype(BF16)


def key_kernel(rows, steps, factor, odd_ref, a, b, x1, s1, x2, s2, x3, s3, am, x1m, s1m, x2m, s2m, x3m, s3m,
               t0_ref, t1_ref, t2_ref, t3_ref, k_ref, gk_ref, rk_ref, dk_ref, dv_ref, tilt, u_acc):
    step = pl.program_id(0)
    heads = steps * PER
    odd = odd_ref[0] == 1
    width = k_ref.shape[1]
    bias = bias_row(
        [jnp.zeros((1, 1), F32), bias_of(am, odd, x1m, s1m), bias_of(am, odd, x2m, s2m), bias_of(am, odd, x3m, s3m)],
        rows,
    )
    scale = 1.0 / math.sqrt(HSIZE)
    pairs = ((b, a), (x1, s1), (x2, s2), (x3, s3))
    stats = (t0_ref, t1_ref, t2_ref, t3_ref)

    @pl.when(step == 0)
    def _():
        u_acc[...] = jnp.zeros_like(u_acc)

    for j in range(PER):
        top = head_rows(j, rows)
        low = head_rows(PER + j, rows)
        head = step * PER + j
        key = jnp.where(odd, a[top, :], b[top, :])
        val = jnp.where(odd, a[low, :], b[low, :])
        queries = jnp.concatenate([jnp.where(odd, o[top, :], e[top, :]) for o, e in pairs], axis=0)
        d_outs = jnp.concatenate([jnp.where(odd, o[low, :], e[low, :]) for o, e in pairs], axis=0)
        log_total = jnp.concatenate([stat[pl.ds(head, 1), :] for stat in stats], axis=1)
        delta = jnp.concatenate([stat[pl.ds(head + heads, 1), :] for stat in stats], axis=1)
        probs = jnp.exp2(dot_nt(key, queries) * factor + (bias - log_total))
        dscores = probs * (dot_nt(val, d_outs) - delta)
        dv_ref[:, head_cols(j)] = dot_nn(probs.astype(BF16), d_outs).astype(BF16)
        cols = pl.ds(pl.multiple_of(head * HSIZE, HSIZE), HSIZE)
        tilted = dot_nn(dscores.astype(BF16), queries) * (scale * gk_ref[pl.ds(head, 1), :])
        tilt[:, cols] = tilted
        u_acc[...] += k_ref[:, cols].astype(F32) * tilted

    @pl.when(step == steps - 1)
    def _():
        rk = rk_ref[...]
        low_part = rk * rk * rk * jnp.sum(u_acc[...], axis=-1, keepdims=True) * (1.0 / width)
        for h in range(heads):
            cols = head_cols(h)
            dk_ref[:, cols] = (rk * tilt[:, cols] - k_ref[:, cols].astype(F32) * low_part).astype(BF16)


def spread_kernel(part_ref, one_ref, two_ref, three_ref, out_ref):
    del one_ref, two_ref, three_ref
    out_ref[...] = jnp.broadcast_to(jnp.sum(part_ref[...].astype(F32), axis=0).astype(BF16)[None], out_ref.shape)


def gains_kernel(part_ref, gq_ref, gk_ref, dq_ref, dk_ref):
    total = jnp.sum(part_ref[...].astype(F32), axis=0)
    dq_ref[...] = total
    dk_ref[...] = total * gq_ref[...] / gk_ref[...]


def params(limit=VMEM_LIMIT):
    return pltpu.CompilerParams(vmem_limit_bytes=limit)


def cost(flops, data=2**20):
    return pl.CostEstimate(flops=flops, bytes_accessed=data, transcendentals=0)


def shape(*dims, dtype=F32):
    return jax.ShapeDtypeStruct(dims, dtype)


def still(*dims):
    return pl.BlockSpec(dims, lambda i, odd: (0,) * len(dims))


def head_blocks(rows, used_if=None):
    def place(i, odd):
        if used_if is None:
            return (i, 0)
        return (i * odd[0] if used_if else i * (1 - odd[0]), 0)

    return pl.BlockSpec((PER * rows, HSIZE), place)


def body(q_in, k_in, v_in, gain_q, gain_k, d_out, video):
    rows, width = q_in.shape
    heads = width // HSIZE
    steps = heads // PER
    factor = math.log2(math.e) / math.sqrt(HSIZE)
    near_by, along = lax.axis_size("dp") * CORES, lax.axis_size("z")
    groups = near_by * along
    odd = lax.axis_index("core").astype(jnp.int32).reshape(1)
    gq = gain_q.reshape(heads, HSIZE)
    gk = gain_k.reshape(heads, HSIZE)
    packed_rows = 2 * heads * rows + MARK_ROWS
    pair_flops = 2 * rows * rows * HSIZE * heads
    smem = pl.BlockSpec(memory_space=pltpu.SMEM)
    vmem = pl.BlockSpec(memory_space=pltpu.VMEM)
    hbm = pl.BlockSpec(memory_space=pl.ANY)

    def after(value, *others):
        return pl.pallas_call(
            gate_kernel,
            out_shape=jax.ShapeDtypeStruct(value.shape, value.dtype),
            in_specs=[hbm] * (1 + len(others)),
            out_specs=hbm,
            input_output_aliases={0: 0},
            compiler_params=params(),
            name="gate",
        )(value, *others)

    def gridded(kernel, name, flops, in_specs, out_specs, out_shape, scratch=()):
        return pl.pallas_call(
            kernel,
            grid_spec=pltpu.PrefetchScalarGridSpec(
                num_scalar_prefetch=1, grid=(steps,), in_specs=in_specs, out_specs=out_specs, scratch_shapes=scratch
            ),
            out_shape=out_shape,
            compiler_params=params(),
            cost_estimate=cost(flops),
            name=name,
        )

    packed = shape(packed_rows, HSIZE, dtype=BF16)
    a, b, rq, rk = pl.pallas_call(
        functools.partial(pack_kernel, heads),
        out_shape=(packed, packed, shape(rows, HSIZE), shape(rows, HSIZE)),
        in_specs=[smem, smem] + [hbm] * 6,
        out_specs=(hbm, hbm, vmem, vmem),
        scratch_shapes=[
            pltpu.VMEM((4, rows, width), BF16),
            pltpu.VMEM((4, heads * rows, HSIZE), BF16),
            pltpu.VMEM((2, heads, HSIZE), F32),
            pltpu.VMEM((MARK_ROWS, HSIZE), BF16),
            pltpu.SemaphoreType.DMA((4, SPLIT + 1)),
            pltpu.SemaphoreType.DMA((4, steps + 1)),
        ],
        compiler_params=params(),
        cost_estimate=cost(pair_flops),
        name="pack",
    )(odd, video, q_in, k_in, d_out, v_in, gq, gk)

    cross = [(i, i + 1) for i in range(1, groups - 1, 2)] + [(i, i - 1) for i in range(2, groups, 2)]
    chip = [(i, i ^ 1) for i in range(groups)]
    x1 = lax.ppermute(a, AXES, cross)
    s1 = lax.ppermute(b, AXES, chip)
    x2 = lax.ppermute(s1, AXES, cross)
    x1 = after(x1, s1)
    s2 = lax.ppermute(x1, AXES, chip)
    x3 = lax.ppermute(s2, AXES, cross)
    x2 = after(x2, s2)
    s3 = lax.ppermute(x2, AXES, chip)

    both = head_blocks(2 * rows)
    if_odd = head_blocks(2 * rows, True)
    if_even = head_blocks(2 * rows, False)
    tall = head_blocks(rows)
    mark = pl.BlockSpec((MARK_ROWS, HSIZE), lambda i, odd: (2 * heads * rows // MARK_ROWS, 0))
    cols = pl.BlockSpec((rows, PER * HSIZE), lambda i, odd: (0, i))
    parts = pl.BlockSpec((1, rows, HSIZE), lambda i, odd: (i, 0, 0))
    square = still(rows, HSIZE)
    whole = still(rows, width)
    near = gridded(
        functools.partial(near_kernel, rows, factor), "near", 1024,
        [both, both, if_even, if_odd, if_even, if_odd] + [mark] * 5,
        (tall, tall, parts),
        (shape(heads * rows, HSIZE), shape(heads * rows, HSIZE), shape(steps, rows, HSIZE)),
    )(odd, a, b, x1, s1, x2, s2, a, x1, s1, x2, s2)
    dq_in, w, stats = gridded(
        functools.partial(query_kernel, rows, steps, factor), "query_side", 1024,
        [if_even, if_odd] + [if_even, if_odd] + [mark] * 3
        + [tall, tall, parts, whole, still(heads, HSIZE), square],
        (whole, still(near_by, heads, HSIZE), still(2 * heads, rows)),
        (shape(rows, width, dtype=BF16), shape(near_by, heads, HSIZE, dtype=BF16), shape(2 * heads, rows)),
        [pltpu.VMEM((rows, HSIZE), F32)] * 3 + [pltpu.VMEM((heads, HSIZE), F32), pltpu.VMEM((rows, width), F32)],
    )(odd, a, b, x3, s3, a, x3, s3, *near, q_in, gq, rq)

    def back(value, by):
        return lax.ppermute(value, AXES, [(i, i - by) for i in range(by, groups)])

    w = lax.all_to_all(w, ("dp", "core"), 0, 0)
    later = [back(stats, by) for by in range(1, WIN)]
    w = pl.pallas_call(
        spread_kernel,
        out_shape=shape(along, heads, HSIZE, dtype=BF16),
        in_specs=[vmem] + [hbm] * 3,
        out_specs=vmem,
        compiler_params=params(),
        cost_estimate=cost(2**20),
        name="spread",
    )(w, *later)
    w = lax.all_to_all(w, "z", 0, 0)
    dgain_q, dgain_k = pl.pallas_call(
        gains_kernel,
        out_shape=(shape(heads, HSIZE),) * 2,
        in_specs=[vmem] * 3,
        out_specs=(vmem,) * 2,
        compiler_params=params(),
        cost_estimate=cost(2**20),
        name="gains",
    )(w, gq, gk)

    dk_in, dv_in = gridded(
        functools.partial(key_kernel, rows, steps, factor), "key_side", 16 * pair_flops,
        [both, both] + [if_odd, if_even] * 3 + [mark] * 7 + [still(2 * heads, rows)] * 4
        + [whole, still(heads, HSIZE), square],
        (whole, cols),
        (shape(rows, width, dtype=BF16),) * 2,
        [pltpu.VMEM((rows, width), F32), pltpu.VMEM((rows, HSIZE), F32)],
    )(odd, a, b, x1, s1, x2, s2, x3, s3, a, x1, s1, x2, s2, x3, s3, stats, *later, k_in, gk, rk)
    return dq_in, dk_in, dv_in, dgain_q.reshape(width), dgain_k.reshape(width)


def solution(mesh):
    dp, seq = mesh.devices.shape
    split = Mesh(mesh.devices.reshape(dp, seq // CORES, CORES), AXES)
    rows = P(AXES, None)
    return jax.shard_map(
        body,
        mesh=split,
        in_specs=(rows, rows, rows, P(), P(), rows, P(AXES)),
        out_specs=(rows, rows, rows, P(), P()),
        check_vma=False,
    )
```

```python
import functools
import math

import jax
import jax.numpy as jnp
from jax import lax
from jax.experimental import pallas as pl
from jax.experimental.pallas import tpu as pltpu
from jax.sharding import Mesh
from jax.sharding import PartitionSpec as P

HSIZE = 128
WIN = 4
EPS = 1e-06
NEG = -1e30
MARK_ROWS = 16
PER = 5
SPLIT = 4
AXES = ("dp", "z", "core")
CORES = 2
VMEM_LIMIT = 63 * 1024 * 1024
F32 = jnp.float32
BF16 = jnp.bfloat16


def dot_nt(a, b):
    return lax.dot_general(a, b, (((1,), (1,)), ((), ())), preferred_element_type=F32)


def dot_nn(a, b):
    return lax.dot_general(a, b, (((1,), (0,)), ((), ())), preferred_element_type=F32)


def head_rows(j, rows):
    return slice(j * rows, (j + 1) * rows)


def head_cols(j):
    return slice(j * HSIZE, (j + 1) * HSIZE)


def pack_kernel(heads, odd_ref, video_ref, q_hbm, k_hbm, d_hbm, v_hbm, gq_hbm, gk_hbm,
                a_hbm, b_hbm, rq_ref, rk_ref, main, stage, gain, mark, in_sems, out_sems):
    odd = odd_ref[0] == 1
    rows, width = q_hbm.shape
    size = rows // SPLIT
    steps = heads // PER
    span = PER * rows

    def load(which, src):
        return [
            pltpu.make_async_copy(
                src.at[pl.ds(part * size, size), :], main.at[which, pl.ds(part * size, size), :], in_sems.at[which, part]
            )
            for part in range(SPLIT)
        ]

    loads = [load(which, src) for which, src in enumerate((q_hbm, k_hbm, d_hbm, v_hbm))]
    gains = [
        pltpu.make_async_copy(src, gain.at[which], in_sems.at[which, SPLIT]) for which, src in enumerate((gq_hbm, gk_hbm))
    ]
    for copy in gains + loads[0] + loads[1] + loads[2] + loads[3]:
        copy.start()

    def store(which, step, dst):
        if step == steps:
            return pltpu.make_async_copy(
                mark, dst.at[pl.ds(2 * steps * span, MARK_ROWS), :], out_sems.at[which, steps]
            )
        return pltpu.make_async_copy(
            stage.at[which, pl.ds(step * span, span), :],
            dst.at[pl.ds((2 * step + which // 2) * span, span), :],
            out_sems.at[which, step],
        )

    def start_store(which, step):
        with_a = odd == (which % 2 == 1)

        @pl.when(with_a)
        def _():
            store(which, step, a_hbm).start()

        @pl.when(jnp.logical_not(with_a))
        def _():
            store(which, step, b_hbm).start()

    mark[...] = jnp.full((MARK_ROWS, HSIZE), (video_ref[0] + 1).astype(F32), F32).astype(BF16)
    for which in range(2):
        start_store(which, steps)
    for copy in gains:
        copy.wait()
    for which, scale_ref in enumerate((rq_ref, rk_ref)):
        for copy in loads[which]:
            copy.wait()
        raw = main[which].astype(F32)
        scale = lax.rsqrt(jnp.sum(raw * raw, axis=-1, keepdims=True) * (1.0 / width) + EPS)
        scale_ref[...] = jnp.broadcast_to(scale, scale_ref.shape)
        for step in range(steps):
            for h in range(step * PER, (step + 1) * PER):
                normed = main[which, :, head_cols(h)].astype(F32) * scale * gain[which, h : h + 1, :]
                stage[which, head_rows(h, rows), :] = normed.astype(BF16)
            start_store(which, step)
    for which in (2, 3):
        for copy in loads[which]:
            copy.wait()
        for step in range(steps):
            for h in range(step * PER, (step + 1) * PER):
                stage[which, head_rows(h, rows), :] = main[which, :, head_cols(h)]
            start_store(which, step)
    for which in range(4):
        for step in range(steps + (which < 2)):
            store(which, step, a_hbm).wait()


def gate_kernel(*refs):
    del refs


def mark_of(ref):
    return ref[0:1, 0:1].astype(F32)


def bias_of(own_ref, odd, if_odd, if_even):
    mark = jnp.where(odd, mark_of(if_odd), mark_of(if_even))
    return jnp.where(mark == mark_of(own_ref), 0.0, NEG)


def bias_row(biases, rows):
    return jnp.concatenate([jnp.broadcast_to(bias, (1, rows)) for bias in biases], axis=1)


def near_kernel(rows, factor, odd_ref, a, b, x1, s1, x2, s2, am, x1m, s1m, x2m, s2m, g_ref, h_ref, part_ref):
    odd = odd_ref[0] == 1
    bias = bias_row([jnp.zeros((1, 1), F32), bias_of(am, odd, s1m, x1m), bias_of(am, odd, s2m, x2m)], rows)
    pairs = ((a, b), (s1, x1), (s2, x2))
    lane = lax.broadcasted_iota(jnp.int32, (rows, HSIZE), 1)
    keys, scores, dprobs = [], [], []
    for j in range(PER):
        top = head_rows(j, rows)
        low = head_rows(PER + j, rows)
        q = jnp.where(odd, b[top, :], a[top, :])
        d_out = jnp.where(odd, b[low, :], a[low, :])
        keys.append(jnp.concatenate([jnp.where(odd, o[top, :], e[top, :]) for o, e in pairs], axis=0))
        vals = jnp.concatenate([jnp.where(odd, o[low, :], e[low, :]) for o, e in pairs], axis=0)
        scores.append(dot_nt(q, keys[j]))
        dprobs.append(dot_nt(d_out, vals))
    part = jnp.zeros((rows, HSIZE), F32)
    for j in range(PER):
        out = head_rows(j, rows)
        score = scores[j] * factor + bias
        best = jnp.max(score, axis=-1, keepdims=True)
        probs = jnp.exp2(score - best)
        total = jnp.sum(probs, axis=-1, keepdims=True)
        delta = jnp.sum(probs * dprobs[j], axis=-1, keepdims=True) / total
        both = jnp.concatenate([(probs * (dprobs[j] - delta)).astype(BF16), probs.astype(BF16)], axis=0)
        sums = dot_nn(both, keys[j])
        g_ref[out, :] = sums[:rows]
        h_ref[out, :] = sums[rows:]
        for place, value in enumerate((best, total, delta)):
            part = jnp.where(lane == 3 * j + place, value, part)
    part_ref[0] = part


def query_kernel(rows, steps, factor, odd_ref, a, b, x3, s3, am, x3m, s3m, g_ref, h_ref, part_ref,
                 q_ref, gq_ref, rq_ref, dq_ref, w_ref, stat_ref, u_acc, acc_lse, acc_delta, acc_w, tilt):
    step = pl.program_id(0)
    heads = steps * PER
    width = q_ref.shape[1]
    odd = odd_ref[0] == 1
    bias = bias_of(am, odd, s3m, x3m)
    rq = rq_ref[...]
    lane = lax.broadcasted_iota(jnp.int32, (rows, HSIZE), 1)
    scale = 1.0 / math.sqrt(HSIZE)

    @pl.when(step == 0)
    def _():
        u_acc[...] = jnp.zeros_like(u_acc)
        acc_lse[...] = jnp.zeros_like(acc_lse)
        acc_delta[...] = jnp.zeros_like(acc_delta)

    keys, scores, dprobs = [], [], []
    for j in range(PER):
        top = head_rows(j, rows)
        low = head_rows(PER + j, rows)
        q = jnp.where(odd, b[top, :], a[top, :])
        d_out = jnp.where(odd, b[low, :], a[low, :])
        keys.append(jnp.where(odd, s3[top, :], x3[top, :]))
        vals = jnp.where(odd, s3[low, :], x3[low, :])
        scores.append(dot_nt(q, keys[j]))
        dprobs.append(dot_nt(d_out, vals))
    lse = acc_lse[...]
    deltas = acc_delta[...]
    fars, nears = [], []
    for j in range(PER):
        old_best, old_total, old_delta = [
            jnp.sum(jnp.where(lane == 3 * j + place, part_ref[0], 0.0), axis=-1, keepdims=True) for place in range(3)
        ]
        score = scores[j] * factor + bias
        best = jnp.maximum(old_best, jnp.max(score, axis=-1, keepdims=True))
        prob = jnp.exp2(score - best)
        shrink = jnp.exp2(old_best - best)
        old_total = old_total * shrink
        total = old_total + jnp.sum(prob, axis=-1, keepdims=True)
        inverse = 1.0 / total
        delta = (old_total * old_delta + jnp.sum(prob * dprobs[j], axis=-1, keepdims=True)) * inverse
        fars.append(((prob * inverse) * (dprobs[j] - delta)).astype(BF16))
        nears.append((shrink * inverse, old_delta - delta))
        head = step * PER + j
        lse = jnp.where(lane == head, best + jnp.log2(total), lse)
        deltas = jnp.where(lane == head, delta, deltas)
    acc_lse[...] = lse
    acc_delta[...] = deltas
    u_sum = u_acc[...]
    for j in range(PER):
        out = head_rows(j, rows)
        head = step * PER + j
        cols = pl.ds(pl.multiple_of(head * HSIZE, HSIZE), HSIZE)
        part, moved = nears[j]
        dq = (dot_nn(fars[j], keys[j]) + part * (g_ref[out, :] + moved * h_ref[out, :])) * scale
        raw = q_ref[:, cols].astype(F32)
        tilted = dq * gq_ref[pl.ds(head, 1), :]
        tilt[:, cols] = tilted
        u_sum = u_sum + raw * tilted
        acc_w[pl.ds(head, 1), :] = jnp.sum(dq * (raw * rq), axis=0, keepdims=True)
    u_acc[...] = u_sum

    @pl.when(step == steps - 1)
    def _():
        stat_ref[:heads, :] = jnp.transpose(acc_lse[...])[:heads, :]
        stat_ref[heads:, :] = jnp.transpose(acc_delta[...])[:heads, :]
        w_ref[...] = jnp.broadcast_to(acc_w[...].astype(BF16)[None], w_ref.shape)
        low_part = rq * rq * rq * jnp.sum(u_sum, axis=-1, keepdims=True) * (1.0 / width)
        for h in range(heads):
            cols = head_cols(h)
            dq_ref[:, cols] = (rq * tilt[:, cols] - q_ref[:, cols].astype(F32) * low_part).astype(BF16)


def key_kernel(rows, steps, factor, odd_ref, a, b, x1, s1, x2, s2, x3, s3, am, x1m, s1m, x2m, s2m, x3m, s3m,
               t0_ref, t1_ref, t2_ref, t3_ref, k_ref, gk_ref, rk_ref, dk_ref, dv_ref, tilt, u_acc):
    step = pl.program_id(0)
    heads = steps * PER
    odd = odd_ref[0] == 1
    width = k_ref.shape[1]
    bias = bias_row(
        [jnp.zeros((1, 1), F32), bias_of(am, odd, x1m, s1m), bias_of(am, odd, x2m, s2m), bias_of(am, odd, x3m, s3m)],
        rows,
    )
    scale = 1.0 / math.sqrt(HSIZE)
    pairs = ((b, a), (x1, s1), (x2, s2), (x3, s3))
    stats = (t0_ref, t1_ref, t2_ref, t3_ref)

    @pl.when(step == 0)
    def _():
        u_acc[...] = jnp.zeros_like(u_acc)

    for j in range(PER):
        top = head_rows(j, rows)
        low = head_rows(PER + j, rows)
        head = step * PER + j
        key = jnp.where(odd, a[top, :], b[top, :])
        val = jnp.where(odd, a[low, :], b[low, :])
        queries = jnp.concatenate([jnp.where(odd, o[top, :], e[top, :]) for o, e in pairs], axis=0)
        d_outs = jnp.concatenate([jnp.where(odd, o[low, :], e[low, :]) for o, e in pairs], axis=0)
        log_total = jnp.concatenate([stat[pl.ds(head, 1), :] for stat in stats], axis=1)
        delta = jnp.concatenate([stat[pl.ds(head + heads, 1), :] for stat in stats], axis=1)
        probs = jnp.exp2(dot_nt(key, queries) * factor + (bias - log_total))
        dscores = probs * (dot_nt(val, d_outs) - delta)
        dv_ref[:, head_cols(j)] = dot_nn(probs.astype(BF16), d_outs).astype(BF16)
        cols = pl.ds(pl.multiple_of(head * HSIZE, HSIZE), HSIZE)
        tilted = dot_nn(dscores.astype(BF16), queries) * (scale * gk_ref[pl.ds(head, 1), :])
        tilt[:, cols] = tilted
        u_acc[...] += k_ref[:, cols].astype(F32) * tilted

    @pl.when(step == steps - 1)
    def _():
        rk = rk_ref[...]
        low_part = rk * rk * rk * jnp.sum(u_acc[...], axis=-1, keepdims=True) * (1.0 / width)
        for h in range(heads):
            cols = head_cols(h)
            dk_ref[:, cols] = (rk * tilt[:, cols] - k_ref[:, cols].astype(F32) * low_part).astype(BF16)


def spread_kernel(part_ref, one_ref, two_ref, three_ref, out_ref):
    del one_ref, two_ref, three_ref
    out_ref[...] = jnp.broadcast_to(jnp.sum(part_ref[...].astype(F32), axis=0).astype(BF16)[None], out_ref.shape)


def gains_kernel(part_ref, gq_ref, gk_ref, dq_ref, dk_ref):
    total = jnp.sum(part_ref[...].astype(F32), axis=0)
    dq_ref[...] = total
    dk_ref[...] = total * gq_ref[...] / gk_ref[...]


def params(limit=VMEM_LIMIT):
    return pltpu.CompilerParams(vmem_limit_bytes=limit)


def cost(flops, data=2**20):
    return pl.CostEstimate(flops=flops, bytes_accessed=data, transcendentals=0)


def shape(*dims, dtype=F32):
    return jax.ShapeDtypeStruct(dims, dtype)


def still(*dims):
    return pl.BlockSpec(dims, lambda i, odd: (0,) * len(dims))


def head_blocks(rows, used_if=None):
    def place(i, odd):
        if used_if is None:
            return (i, 0)
        return (i * odd[0] if used_if else i * (1 - odd[0]), 0)

    return pl.BlockSpec((PER * rows, HSIZE), place)


def body(q_in, k_in, v_in, gain_q, gain_k, d_out, video):
    rows, width = q_in.shape
    heads = width // HSIZE
    steps = heads // PER
    factor = math.log2(math.e) / math.sqrt(HSIZE)
    near_by, along = lax.axis_size("dp") * CORES, lax.axis_size("z")
    groups = near_by * along
    odd = lax.axis_index("core").astype(jnp.int32).reshape(1)
    gq = gain_q.reshape(heads, HSIZE)
    gk = gain_k.reshape(heads, HSIZE)
    packed_rows = 2 * heads * rows + MARK_ROWS
    pair_flops = 2 * rows * rows * HSIZE * heads
    smem = pl.BlockSpec(memory_space=pltpu.SMEM)
    vmem = pl.BlockSpec(memory_space=pltpu.VMEM)
    hbm = pl.BlockSpec(memory_space=pl.ANY)

    def after(value, *others):
        return pl.pallas_call(
            gate_kernel,
            out_shape=jax.ShapeDtypeStruct(value.shape, value.dtype),
            in_specs=[hbm] * (1 + len(others)),
            out_specs=hbm,
            input_output_aliases={0: 0},
            compiler_params=params(),
            name="gate",
        )(value, *others)

    def gridded(kernel, name, flops, in_specs, out_specs, out_shape, scratch=()):
        return pl.pallas_call(
            kernel,
            grid_spec=pltpu.PrefetchScalarGridSpec(
                num_scalar_prefetch=1, grid=(steps,), in_specs=in_specs, out_specs=out_specs, scratch_shapes=scratch
            ),
            out_shape=out_shape,
            compiler_params=params(),
            cost_estimate=cost(flops),
            name=name,
        )

    packed = shape(packed_rows, HSIZE, dtype=BF16)
    a, b, rq, rk = pl.pallas_call(
        functools.partial(pack_kernel, heads),
        out_shape=(packed, packed, shape(rows, HSIZE), shape(rows, HSIZE)),
        in_specs=[smem, smem] + [hbm] * 6,
        out_specs=(hbm, hbm, vmem, vmem),
        scratch_shapes=[
            pltpu.VMEM((4, rows, width), BF16),
            pltpu.VMEM((4, heads * rows, HSIZE), BF16),
            pltpu.VMEM((2, heads, HSIZE), F32),
            pltpu.VMEM((MARK_ROWS, HSIZE), BF16),
            pltpu.SemaphoreType.DMA((4, SPLIT + 1)),
            pltpu.SemaphoreType.DMA((4, steps + 1)),
        ],
        compiler_params=params(),
        cost_estimate=cost(pair_flops),
        name="pack",
    )(odd, video, q_in, k_in, d_out, v_in, gq, gk)

    cross = [(i, i + 1) for i in range(1, groups - 1, 2)] + [(i, i - 1) for i in range(2, groups, 2)]
    chip = [(i, i ^ 1) for i in range(groups)]
    next_chip = [(i, i + 2) for i in range(0, groups - 2, 2)] + [(i, i - 2) for i in range(3, groups, 2)]
    x1 = lax.ppermute(a, AXES, cross)
    s1 = lax.ppermute(b, AXES, chip)
    x2 = lax.ppermute(s1, AXES, cross)
    x3 = lax.ppermute(x1, AXES, next_chip)
    s2 = lax.ppermute(x1, AXES, chip)
    s3 = lax.ppermute(x2, AXES, chip)

    both = head_blocks(2 * rows)
    if_odd = head_blocks(2 * rows, True)
    if_even = head_blocks(2 * rows, False)
    tall = head_blocks(rows)
    mark = pl.BlockSpec((MARK_ROWS, HSIZE), lambda i, odd: (2 * heads * rows // MARK_ROWS, 0))
    cols = pl.BlockSpec((rows, PER * HSIZE), lambda i, odd: (0, i))
    parts = pl.BlockSpec((1, rows, HSIZE), lambda i, odd: (i, 0, 0))
    square = still(rows, HSIZE)
    whole = still(rows, width)
    near = gridded(
        functools.partial(near_kernel, rows, factor), "near", 1024,
        [both, both, if_even, if_odd, if_even, if_odd] + [mark] * 5,
        (tall, tall, parts),
        (shape(heads * rows, HSIZE), shape(heads * rows, HSIZE), shape(steps, rows, HSIZE)),
    )(odd, a, b, x1, s1, x2, s2, a, x1, s1, x2, s2)
    dq_in, w, stats = gridded(
        functools.partial(query_kernel, rows, steps, factor), "query_side", 1024,
        [if_even, if_odd] + [if_even, if_odd] + [mark] * 3
        + [tall, tall, parts, whole, still(heads, HSIZE), square],
        (whole, still(near_by, heads, HSIZE), still(2 * heads, rows)),
        (shape(rows, width, dtype=BF16), shape(near_by, heads, HSIZE, dtype=BF16), shape(2 * heads, rows)),
        [pltpu.VMEM((rows, HSIZE), F32)] * 3 + [pltpu.VMEM((heads, HSIZE), F32), pltpu.VMEM((rows, width), F32)],
    )(odd, a, b, x3, s3, a, x3, s3, *near, q_in, gq, rq)

    def back(value, by):
        return lax.ppermute(value, AXES, [(i, i - by) for i in range(by, groups)])

    w = lax.all_to_all(w, ("dp", "core"), 0, 0)
    later = [back(stats, by) for by in range(1, WIN)]
    w = pl.pallas_call(
        spread_kernel,
        out_shape=shape(along, heads, HSIZE, dtype=BF16),
        in_specs=[vmem] + [hbm] * 3,
        out_specs=vmem,
        compiler_params=params(),
        cost_estimate=cost(2**20),
        name="spread",
    )(w, *later)
    w = lax.all_to_all(w, "z", 0, 0)
    dgain_q, dgain_k = pl.pallas_call(
        gains_kernel,
        out_shape=(shape(heads, HSIZE),) * 2,
        in_specs=[vmem] * 3,
        out_specs=(vmem,) * 2,
        compiler_params=params(),
        cost_estimate=cost(2**20),
        name="gains",
    )(w, gq, gk)

    dk_in, dv_in = gridded(
        functools.partial(key_kernel, rows, steps, factor), "key_side", 16 * pair_flops,
        [both, both] + [if_odd, if_even] * 3 + [mark] * 7 + [still(2 * heads, rows)] * 4
        + [whole, still(heads, HSIZE), square],
        (whole, cols),
        (shape(rows, width, dtype=BF16),) * 2,
        [pltpu.VMEM((rows, width), F32), pltpu.VMEM((rows, HSIZE), F32)],
    )(odd, a, b, x1, s1, x2, s2, x3, s3, a, x1, s1, x2, s2, x3, s3, stats, *later, k_in, gk, rk)
    return dq_in, dk_in, dv_in, dgain_q.reshape(width), dgain_k.reshape(width)


def solution(mesh):
    dp, seq = mesh.devices.shape
    split = Mesh(mesh.devices.reshape(dp, seq // CORES, CORES), AXES)
    rows = P(AXES, None)
    return jax.shard_map(
        body,
        mesh=split,
        in_specs=(rows, rows, rows, P(), P(), rows, P(AXES)),
        out_specs=(rows, rows, rows, P(), P()),
        check_vma=False,
    )
```

```python
import functools
import math

import jax
import jax.numpy as jnp
from jax import lax
from jax.experimental import pallas as pl
from jax.experimental.pallas import tpu as pltpu
from jax.sharding import Mesh
from jax.sharding import PartitionSpec as P

HSIZE = 128
WIN = 4
EPS = 1e-06
NEG = -1e30
MARK_ROWS = 16
PER = 5
SPLIT = 4
AXES = ("dp", "z", "core")
CORES = 2
VMEM_LIMIT = 63 * 1024 * 1024
SMALL_LIMIT = 8 * 1024 * 1024
F32 = jnp.float32
BF16 = jnp.bfloat16


def dot_nt(a, b):
    return lax.dot_general(a, b, (((1,), (1,)), ((), ())), preferred_element_type=F32)


def dot_nn(a, b):
    return lax.dot_general(a, b, (((1,), (0,)), ((), ())), preferred_element_type=F32)


def head_rows(j, rows):
    return slice(j * rows, (j + 1) * rows)


def head_cols(j):
    return slice(j * HSIZE, (j + 1) * HSIZE)


def pack_kernel(heads, odd_ref, video_ref, q_hbm, k_hbm, d_hbm, v_hbm, gq_hbm, gk_hbm,
                a_hbm, b_hbm, rq_ref, rk_ref, main, stage, gain, mark, in_sems, out_sems):
    odd = odd_ref[0] == 1
    rows, width = q_hbm.shape
    size = rows // SPLIT
    steps = heads // PER
    span = PER * rows

    def load(which, src):
        return [
            pltpu.make_async_copy(
                src.at[pl.ds(part * size, size), :], main.at[which, pl.ds(part * size, size), :], in_sems.at[which, part]
            )
            for part in range(SPLIT)
        ]

    loads = [load(which, src) for which, src in enumerate((q_hbm, k_hbm, d_hbm, v_hbm))]
    gains = [
        pltpu.make_async_copy(src, gain.at[which], in_sems.at[which, SPLIT]) for which, src in enumerate((gq_hbm, gk_hbm))
    ]
    for copy in gains + loads[0] + loads[1] + loads[2] + loads[3]:
        copy.start()

    def store(which, step, dst):
        if step == steps:
            return pltpu.make_async_copy(
                mark, dst.at[pl.ds(2 * steps * span, MARK_ROWS), :], out_sems.at[which, steps]
            )
        return pltpu.make_async_copy(
            stage.at[which, pl.ds(step * span, span), :],
            dst.at[pl.ds((2 * step + which // 2) * span, span), :],
            out_sems.at[which, step],
        )

    def start_store(which, step):
        with_a = odd == (which % 2 == 1)

        @pl.when(with_a)
        def _():
            store(which, step, a_hbm).start()

        @pl.when(jnp.logical_not(with_a))
        def _():
            store(which, step, b_hbm).start()

    mark[...] = jnp.full((MARK_ROWS, HSIZE), (video_ref[0] + 1).astype(F32), F32).astype(BF16)
    for which in range(2):
        start_store(which, steps)
    for copy in gains:
        copy.wait()
    for which, scale_ref in enumerate((rq_ref, rk_ref)):
        for copy in loads[which]:
            copy.wait()
        raw = main[which].astype(F32)
        scale = lax.rsqrt(jnp.sum(raw * raw, axis=-1, keepdims=True) * (1.0 / width) + EPS)
        scale_ref[...] = jnp.broadcast_to(scale, scale_ref.shape)
        for step in range(steps):
            for h in range(step * PER, (step + 1) * PER):
                normed = main[which, :, head_cols(h)].astype(F32) * scale * gain[which, h : h + 1, :]
                stage[which, head_rows(h, rows), :] = normed.astype(BF16)
            start_store(which, step)
    for which in (2, 3):
        for copy in loads[which]:
            copy.wait()
        for step in range(steps):
            for h in range(step * PER, (step + 1) * PER):
                stage[which, head_rows(h, rows), :] = main[which, :, head_cols(h)]
            start_store(which, step)
    for which in range(4):
        for step in range(steps + (which < 2)):
            store(which, step, a_hbm).wait()


def gate_kernel(*refs):
    del refs


def mark_of(ref):
    return ref[0:1, 0:1].astype(F32)


def bias_of(own_ref, odd, if_odd, if_even):
    mark = jnp.where(odd, mark_of(if_odd), mark_of(if_even))
    return jnp.where(mark == mark_of(own_ref), 0.0, NEG)


def bias_row(biases, rows):
    return jnp.concatenate([jnp.broadcast_to(bias, (1, rows)) for bias in biases], axis=1)


def near_kernel(rows, factor, odd_ref, a, b, x1, s1, x2, s2, am, x1m, s1m, x2m, s2m, g_ref, h_ref, part_ref):
    odd = odd_ref[0] == 1
    bias = bias_row([jnp.zeros((1, 1), F32), bias_of(am, odd, s1m, x1m), bias_of(am, odd, s2m, x2m)], rows)
    pairs = ((a, b), (s1, x1), (s2, x2))
    lane = lax.broadcasted_iota(jnp.int32, (rows, HSIZE), 1)
    keys, scores, dprobs = [], [], []
    for j in range(PER):
        top = head_rows(j, rows)
        low = head_rows(PER + j, rows)
        q = jnp.where(odd, b[top, :], a[top, :])
        d_out = jnp.where(odd, b[low, :], a[low, :])
        keys.append(jnp.concatenate([jnp.where(odd, o[top, :], e[top, :]) for o, e in pairs], axis=0))
        vals = jnp.concatenate([jnp.where(odd, o[low, :], e[low, :]) for o, e in pairs], axis=0)
        scores.append(dot_nt(q, keys[j]))
        dprobs.append(dot_nt(d_out, vals))
    part = jnp.zeros((rows, HSIZE), F32)
    for j in range(PER):
        out = head_rows(j, rows)
        score = scores[j] * factor + bias
        best = jnp.max(score, axis=-1, keepdims=True)
        probs = jnp.exp2(score - best)
        total = jnp.sum(probs, axis=-1, keepdims=True)
        delta = jnp.sum(probs * dprobs[j], axis=-1, keepdims=True) / total
        both = jnp.concatenate([(probs * (dprobs[j] - delta)).astype(BF16), probs.astype(BF16)], axis=0)
        sums = dot_nn(both, keys[j])
        g_ref[out, :] = sums[:rows]
        h_ref[out, :] = sums[rows:]
        for place, value in enumerate((best, total, delta)):
            part = jnp.where(lane == 3 * j + place, value, part)
    part_ref[0] = part


def query_kernel(rows, steps, factor, odd_ref, a, b, x3, s3, am, x3m, s3m, g_ref, h_ref, part_ref,
                 q_ref, gq_ref, rq_ref, dq_ref, w_ref, stat_ref, u_acc, acc_lse, acc_delta, acc_w, tilt):
    step = pl.program_id(0)
    heads = steps * PER
    width = q_ref.shape[1]
    odd = odd_ref[0] == 1
    bias = bias_of(am, odd, s3m, x3m)
    rq = rq_ref[...]
    lane = lax.broadcasted_iota(jnp.int32, (rows, HSIZE), 1)
    scale = 1.0 / math.sqrt(HSIZE)

    @pl.when(step == 0)
    def _():
        u_acc[...] = jnp.zeros_like(u_acc)
        acc_lse[...] = jnp.zeros_like(acc_lse)
        acc_delta[...] = jnp.zeros_like(acc_delta)

    keys, scores, dprobs = [], [], []
    for j in range(PER):
        top = head_rows(j, rows)
        low = head_rows(PER + j, rows)
        q = jnp.where(odd, b[top, :], a[top, :])
        d_out = jnp.where(odd, b[low, :], a[low, :])
        keys.append(jnp.where(odd, s3[top, :], x3[top, :]))
        vals = jnp.where(odd, s3[low, :], x3[low, :])
        scores.append(dot_nt(q, keys[j]))
        dprobs.append(dot_nt(d_out, vals))
    lse = acc_lse[...]
    deltas = acc_delta[...]
    fars, nears = [], []
    for j in range(PER):
        old_best, old_total, old_delta = [
            jnp.sum(jnp.where(lane == 3 * j + place, part_ref[0], 0.0), axis=-1, keepdims=True) for place in range(3)
        ]
        score = scores[j] * factor + bias
        best = jnp.maximum(old_best, jnp.max(score, axis=-1, keepdims=True))
        prob = jnp.exp2(score - best)
        shrink = jnp.exp2(old_best - best)
        old_total = old_total * shrink
        total = old_total + jnp.sum(prob, axis=-1, keepdims=True)
        inverse = 1.0 / total
        delta = (old_total * old_delta + jnp.sum(prob * dprobs[j], axis=-1, keepdims=True)) * inverse
        fars.append(((prob * inverse) * (dprobs[j] - delta)).astype(BF16))
        nears.append((shrink * inverse, old_delta - delta))
        head = step * PER + j
        lse = jnp.where(lane == head, best + jnp.log2(total), lse)
        deltas = jnp.where(lane == head, delta, deltas)
    acc_lse[...] = lse
    acc_delta[...] = deltas
    u_sum = u_acc[...]
    for j in range(PER):
        out = head_rows(j, rows)
        head = step * PER + j
        cols = pl.ds(pl.multiple_of(head * HSIZE, HSIZE), HSIZE)
        part, moved = nears[j]
        dq = (dot_nn(fars[j], keys[j]) + part * (g_ref[out, :] + moved * h_ref[out, :])) * scale
        raw = q_ref[:, cols].astype(F32)
        tilted = dq * gq_ref[pl.ds(head, 1), :]
        tilt[:, cols] = tilted
        u_sum = u_sum + raw * tilted
        acc_w[pl.ds(head, 1), :] = jnp.sum(dq * (raw * rq), axis=0, keepdims=True)
    u_acc[...] = u_sum

    @pl.when(step == steps - 1)
    def _():
        stat_ref[:heads, :] = jnp.transpose(acc_lse[...])[:heads, :]
        stat_ref[heads:, :] = jnp.transpose(acc_delta[...])[:heads, :]
        w_ref[...] = jnp.broadcast_to(acc_w[...].astype(BF16)[None], w_ref.shape)
        low_part = rq * rq * rq * jnp.sum(u_sum, axis=-1, keepdims=True) * (1.0 / width)
        for h in range(heads):
            cols = head_cols(h)
            dq_ref[:, cols] = (rq * tilt[:, cols] - q_ref[:, cols].astype(F32) * low_part).astype(BF16)


def key_kernel(rows, steps, factor, odd_ref, a, b, x1, s1, x2, s2, x3, s3, am, x1m, s1m, x2m, s2m, x3m, s3m,
               t0_ref, t1_ref, t2_ref, t3_ref, k_ref, gk_ref, rk_ref, dk_ref, dv_ref, tilt, u_acc):
    step = pl.program_id(0)
    heads = steps * PER
    odd = odd_ref[0] == 1
    width = k_ref.shape[1]
    bias = bias_row(
        [jnp.zeros((1, 1), F32), bias_of(am, odd, x1m, s1m), bias_of(am, odd, x2m, s2m), bias_of(am, odd, x3m, s3m)],
        rows,
    )
    scale = 1.0 / math.sqrt(HSIZE)
    pairs = ((b, a), (x1, s1), (x2, s2), (x3, s3))
    stats = (t0_ref, t1_ref, t2_ref, t3_ref)

    @pl.when(step == 0)
    def _():
        u_acc[...] = jnp.zeros_like(u_acc)

    for j in range(PER):
        top = head_rows(j, rows)
        low = head_rows(PER + j, rows)
        head = step * PER + j
        key = jnp.where(odd, a[top, :], b[top, :])
        val = jnp.where(odd, a[low, :], b[low, :])
        queries = jnp.concatenate([jnp.where(odd, o[top, :], e[top, :]) for o, e in pairs], axis=0)
        d_outs = jnp.concatenate([jnp.where(odd, o[low, :], e[low, :]) for o, e in pairs], axis=0)
        log_total = jnp.concatenate([stat[pl.ds(head, 1), :] for stat in stats], axis=1)
        delta = jnp.concatenate([stat[pl.ds(head + heads, 1), :] for stat in stats], axis=1)
        probs = jnp.exp2(dot_nt(key, queries) * factor + (bias - log_total))
        dscores = probs * (dot_nt(val, d_outs) - delta)
        dv_ref[:, head_cols(j)] = dot_nn(probs.astype(BF16), d_outs).astype(BF16)
        cols = pl.ds(pl.multiple_of(head * HSIZE, HSIZE), HSIZE)
        tilted = dot_nn(dscores.astype(BF16), queries) * (scale * gk_ref[pl.ds(head, 1), :])
        tilt[:, cols] = tilted
        u_acc[...] += k_ref[:, cols].astype(F32) * tilted

    @pl.when(step == steps - 1)
    def _():
        rk = rk_ref[...]
        low_part = rk * rk * rk * jnp.sum(u_acc[...], axis=-1, keepdims=True) * (1.0 / width)
        for h in range(heads):
            cols = head_cols(h)
            dk_ref[:, cols] = (rk * tilt[:, cols] - k_ref[:, cols].astype(F32) * low_part).astype(BF16)


def spread_kernel(part_ref, one_ref, two_ref, three_ref, out_ref):
    del one_ref, two_ref, three_ref
    out_ref[...] = jnp.broadcast_to(jnp.sum(part_ref[...].astype(F32), axis=0).astype(BF16)[None], out_ref.shape)


def gains_kernel(part_ref, gq_ref, gk_ref, dq_ref, dk_ref):
    total = jnp.sum(part_ref[...].astype(F32), axis=0)
    dq_ref[...] = total
    dk_ref[...] = total * gq_ref[...] / gk_ref[...]


def params(limit=VMEM_LIMIT):
    return pltpu.CompilerParams(vmem_limit_bytes=limit)


def cost(flops, data=2**20):
    return pl.CostEstimate(flops=flops, bytes_accessed=data, transcendentals=0)


def shape(*dims, dtype=F32):
    return jax.ShapeDtypeStruct(dims, dtype)


def still(*dims):
    return pl.BlockSpec(dims, lambda i, odd: (0,) * len(dims))


def head_blocks(rows, used_if=None):
    def place(i, odd):
        if used_if is None:
            return (i, 0)
        return (i * odd[0] if used_if else i * (1 - odd[0]), 0)

    return pl.BlockSpec((PER * rows, HSIZE), place)


def body(q_in, k_in, v_in, gain_q, gain_k, d_out, video):
    rows, width = q_in.shape
    heads = width // HSIZE
    steps = heads // PER
    factor = math.log2(math.e) / math.sqrt(HSIZE)
    near_by, along = lax.axis_size("dp") * CORES, lax.axis_size("z")
    groups = near_by * along
    odd = lax.axis_index("core").astype(jnp.int32).reshape(1)
    gq = gain_q.reshape(heads, HSIZE)
    gk = gain_k.reshape(heads, HSIZE)
    packed_rows = 2 * heads * rows + MARK_ROWS
    pair_flops = 2 * rows * rows * HSIZE * heads
    smem = pl.BlockSpec(memory_space=pltpu.SMEM)
    vmem = pl.BlockSpec(memory_space=pltpu.VMEM)
    hbm = pl.BlockSpec(memory_space=pl.ANY)

    def after(value, *others):
        return pl.pallas_call(
            gate_kernel,
            out_shape=jax.ShapeDtypeStruct(value.shape, value.dtype),
            in_specs=[hbm] * (1 + len(others)),
            out_specs=hbm,
            input_output_aliases={0: 0},
            compiler_params=params(),
            name="gate",
        )(value, *others)

    def gridded(kernel, name, flops, in_specs, out_specs, out_shape, scratch=(), limit=VMEM_LIMIT):
        return pl.pallas_call(
            kernel,
            grid_spec=pltpu.PrefetchScalarGridSpec(
                num_scalar_prefetch=1, grid=(steps,), in_specs=in_specs, out_specs=out_specs, scratch_shapes=scratch
            ),
            out_shape=out_shape,
            compiler_params=params(limit),
            cost_estimate=cost(flops),
            name=name,
        )

    packed = shape(packed_rows, HSIZE, dtype=BF16)
    a, b, rq, rk = pl.pallas_call(
        functools.partial(pack_kernel, heads),
        out_shape=(packed, packed, shape(rows, HSIZE), shape(rows, HSIZE)),
        in_specs=[smem, smem] + [hbm] * 6,
        out_specs=(hbm, hbm, vmem, vmem),
        scratch_shapes=[
            pltpu.VMEM((4, rows, width), BF16),
            pltpu.VMEM((4, heads * rows, HSIZE), BF16),
            pltpu.VMEM((2, heads, HSIZE), F32),
            pltpu.VMEM((MARK_ROWS, HSIZE), BF16),
            pltpu.SemaphoreType.DMA((4, SPLIT + 1)),
            pltpu.SemaphoreType.DMA((4, steps + 1)),
        ],
        compiler_params=params(),
        cost_estimate=cost(pair_flops),
        name="pack",
    )(odd, video, q_in, k_in, d_out, v_in, gq, gk)

    cross = [(i, i + 1) for i in range(1, groups - 1, 2)] + [(i, i - 1) for i in range(2, groups, 2)]
    chip = [(i, i ^ 1) for i in range(groups)]
    next_chip = [(i, i + 2) for i in range(0, groups - 2, 2)] + [(i, i - 2) for i in range(3, groups, 2)]
    x1 = lax.ppermute(a, AXES, cross)
    s1 = lax.ppermute(b, AXES, chip)
    x2 = lax.ppermute(s1, AXES, cross)
    x3 = lax.ppermute(x1, AXES, next_chip)
    s2 = lax.ppermute(x1, AXES, chip)
    s3 = lax.ppermute(x2, AXES, chip)

    both = head_blocks(2 * rows)
    if_odd = head_blocks(2 * rows, True)
    if_even = head_blocks(2 * rows, False)
    tall = head_blocks(rows)
    mark = pl.BlockSpec((MARK_ROWS, HSIZE), lambda i, odd: (2 * heads * rows // MARK_ROWS, 0))
    cols = pl.BlockSpec((rows, PER * HSIZE), lambda i, odd: (0, i))
    parts = pl.BlockSpec((1, rows, HSIZE), lambda i, odd: (i, 0, 0))
    square = still(rows, HSIZE)
    whole = still(rows, width)
    near = gridded(
        functools.partial(near_kernel, rows, factor), "near", 1024,
        [both, both, if_even, if_odd, if_even, if_odd] + [mark] * 5,
        (tall, tall, parts),
        (shape(heads * rows, HSIZE), shape(heads * rows, HSIZE), shape(steps, rows, HSIZE)),
    )(odd, a, b, x1, s1, x2, s2, a, x1, s1, x2, s2)
    dq_in, w, stats = gridded(
        functools.partial(query_kernel, rows, steps, factor), "query_side", 1024,
        [if_even, if_odd] + [if_even, if_odd] + [mark] * 3
        + [tall, tall, parts, whole, still(heads, HSIZE), square],
        (whole, still(along, heads, HSIZE), still(2 * heads, rows)),
        (shape(rows, width, dtype=BF16), shape(along, heads, HSIZE, dtype=BF16), shape(2 * heads, rows)),
        [pltpu.VMEM((rows, HSIZE), F32)] * 3 + [pltpu.VMEM((heads, HSIZE), F32), pltpu.VMEM((rows, width), F32)],
    )(odd, a, b, x3, s3, a, x3, s3, *near, q_in, gq, rq)

    def back(value, by):
        return lax.ppermute(value, AXES, [(i, i - by) for i in range(by, groups)])

    w = lax.all_to_all(w, "z", 0, 0)
    later = [back(stats, by) for by in range(1, WIN)]
    w = pl.pallas_call(
        spread_kernel,
        out_shape=shape(near_by, heads, HSIZE, dtype=BF16),
        in_specs=[vmem] + [hbm] * 3,
        out_specs=vmem,
        compiler_params=params(SMALL_LIMIT),
        cost_estimate=cost(2**20),
        name="spread",
    )(w, *later)
    w = lax.all_to_all(w, ("dp", "core"), 0, 0)
    dgain_q, dgain_k = pl.pallas_call(
        gains_kernel,
        out_shape=(shape(heads, HSIZE),) * 2,
        in_specs=[vmem] * 3,
        out_specs=(vmem,) * 2,
        compiler_params=params(SMALL_LIMIT),
        cost_estimate=cost(2**20),
        name="gains",
    )(w, gq, gk)

    dk_in, dv_in = gridded(
        functools.partial(key_kernel, rows, steps, factor), "key_side", 16 * pair_flops,
        [both, both] + [if_odd, if_even] * 3 + [mark] * 7 + [still(2 * heads, rows)] * 4
        + [whole, still(heads, HSIZE), square],
        (whole, cols),
        (shape(rows, width, dtype=BF16),) * 2,
        [pltpu.VMEM((rows, width), F32), pltpu.VMEM((rows, HSIZE), F32)],
        62 * 1024 * 1024,
    )(odd, a, b, x1, s1, x2, s2, x3, s3, a, x1, s1, x2, s2, x3, s3, stats, *later, k_in, gk, rk)
    return dq_in, dk_in, dv_in, dgain_q.reshape(width), dgain_k.reshape(width)


def solution(mesh):
    dp, seq = mesh.devices.shape
    split = Mesh(mesh.devices.reshape(dp, seq // CORES, CORES), AXES)
    rows = P(AXES, None)
    return jax.shard_map(
        body,
        mesh=split,
        in_specs=(rows, rows, rows, P(), P(), rows, P(AXES)),
        out_specs=(rows, rows, rows, P(), P()),
        check_vma=False,
    )
```

```python
import functools
import math

import jax
import jax.numpy as jnp
from jax import lax
from jax.experimental import pallas as pl
from jax.experimental.pallas import tpu as pltpu
from jax.sharding import Mesh
from jax.sharding import PartitionSpec as P

HSIZE = 128
WIN = 4
EPS = 1e-06
NEG = -1e30
MARK_ROWS = 16
PER = 5
SPLIT = 4
AXES = ("dp", "z", "core")
CORES = 2
VMEM_LIMIT = 63 * 1024 * 1024
SMALL_LIMIT = 8 * 1024 * 1024
KEY_LIMIT = 62 * 1024 * 1024
F32 = jnp.float32
BF16 = jnp.bfloat16


def dot_nt(a, b):
    return lax.dot_general(a, b, (((1,), (1,)), ((), ())), preferred_element_type=F32)


def dot_nn(a, b):
    return lax.dot_general(a, b, (((1,), (0,)), ((), ())), preferred_element_type=F32)


def head_rows(j, rows):
    return slice(j * rows, (j + 1) * rows)


def head_cols(j):
    return slice(j * HSIZE, (j + 1) * HSIZE)


def pack_kernel(heads, odd_ref, video_ref, q_hbm, k_hbm, d_hbm, v_hbm, gq_hbm, gk_hbm,
                a_hbm, b_hbm, rq_hbm, rk_hbm, main, stage, gain, mark, scales, in_sems, out_sems):
    odd = odd_ref[0] == 1
    rows, width = q_hbm.shape
    size = rows // SPLIT
    steps = heads // PER
    span = PER * rows

    def load(which, src):
        return [
            pltpu.make_async_copy(
                src.at[pl.ds(part * size, size), :], main.at[which, pl.ds(part * size, size), :], in_sems.at[which, part]
            )
            for part in range(SPLIT)
        ]

    loads = [load(which, src) for which, src in enumerate((q_hbm, k_hbm, d_hbm, v_hbm))]
    gains = [
        pltpu.make_async_copy(src, gain.at[which], in_sems.at[which, SPLIT]) for which, src in enumerate((gq_hbm, gk_hbm))
    ]
    for copy in gains + loads[0] + loads[1] + loads[2] + loads[3]:
        copy.start()

    def store(which, step, dst):
        if step == steps:
            return pltpu.make_async_copy(
                mark, dst.at[pl.ds(2 * steps * span, MARK_ROWS), :], out_sems.at[which, steps]
            )
        return pltpu.make_async_copy(
            stage.at[which, pl.ds(step * span, span), :],
            dst.at[pl.ds((2 * step + which // 2) * span, span), :],
            out_sems.at[which, step],
        )

    def start_store(which, step):
        with_a = odd == (which % 2 == 1)

        @pl.when(with_a)
        def _():
            store(which, step, a_hbm).start()

        @pl.when(jnp.logical_not(with_a))
        def _():
            store(which, step, b_hbm).start()

    mark[...] = jnp.full((MARK_ROWS, HSIZE), (video_ref[0] + 1).astype(F32), F32).astype(BF16)
    for which in range(2):
        start_store(which, steps)
    for copy in gains:
        copy.wait()
    scale_stores = [
        pltpu.make_async_copy(scales.at[which], dst, out_sems.at[2 + which, steps])
        for which, dst in enumerate((rq_hbm, rk_hbm))
    ]
    for which in range(2):
        for copy in loads[which]:
            copy.wait()
        raw = main[which].astype(F32)
        scale = lax.rsqrt(jnp.sum(raw * raw, axis=-1, keepdims=True) * (1.0 / width) + EPS)
        scales[which] = jnp.broadcast_to(scale, (rows, HSIZE))
        scale_stores[which].start()
        for step in range(steps):
            for h in range(step * PER, (step + 1) * PER):
                normed = main[which, :, head_cols(h)].astype(F32) * scale * gain[which, h : h + 1, :]
                stage[which, head_rows(h, rows), :] = normed.astype(BF16)
            start_store(which, step)
    for which in (2, 3):
        for copy in loads[which]:
            copy.wait()
        for step in range(steps):
            for h in range(step * PER, (step + 1) * PER):
                stage[which, head_rows(h, rows), :] = main[which, :, head_cols(h)]
            start_store(which, step)
    for which in range(4):
        for step in range(steps + (which < 2)):
            store(which, step, a_hbm).wait()
    for copy in scale_stores:
        copy.wait()


def mark_of(ref):
    return ref[0:1, 0:1].astype(F32)


def bias_of(own_ref, odd, if_odd, if_even):
    mark = jnp.where(odd, mark_of(if_odd), mark_of(if_even))
    return jnp.where(mark == mark_of(own_ref), 0.0, NEG)


def bias_row(biases, rows):
    return jnp.concatenate([jnp.broadcast_to(bias, (1, rows)) for bias in biases], axis=1)


def near_kernel(rows, factor, odd_ref, a, b, x1, s1, x2, s2, am, x1m, s1m, x2m, s2m, g_ref, h_ref, stat_ref):
    odd = odd_ref[0] == 1
    bias = bias_row([jnp.zeros((1, 1), F32), bias_of(am, odd, s1m, x1m), bias_of(am, odd, s2m, x2m)], rows)
    pairs = ((a, b), (s1, x1), (s2, x2))
    left = lax.broadcasted_iota(jnp.int32, (rows, HSIZE), 1) < HSIZE // 2
    keys, scores, dprobs = [], [], []
    for j in range(PER):
        top = head_rows(j, rows)
        low = head_rows(PER + j, rows)
        q = jnp.where(odd, b[top, :], a[top, :])
        d_out = jnp.where(odd, b[low, :], a[low, :])
        keys.append(jnp.concatenate([jnp.where(odd, o[top, :], e[top, :]) for o, e in pairs], axis=0))
        vals = jnp.concatenate([jnp.where(odd, o[low, :], e[low, :]) for o, e in pairs], axis=0)
        scores.append(dot_nt(q, keys[j]))
        dprobs.append(dot_nt(d_out, vals))
    for j in range(PER):
        out = head_rows(j, rows)
        score = scores[j] * factor + bias
        best = jnp.max(score, axis=-1, keepdims=True)
        probs = jnp.exp2(score - best)
        total = jnp.sum(probs, axis=-1, keepdims=True)
        inverse = 1.0 / total
        probs = probs * inverse
        delta = jnp.sum(probs * dprobs[j], axis=-1, keepdims=True)
        both = jnp.concatenate([(probs * (dprobs[j] - delta)).astype(BF16), probs.astype(BF16)], axis=0)
        sums = dot_nn(both, keys[j])
        g_ref[out, :] = sums[:rows]
        h_ref[out, :] = sums[rows:]
        stat_ref[out, :] = jnp.where(left, best + jnp.log2(total), delta)


class Loads:
    def __init__(self, odd, sems):
        self.odd, self.sems, self.taken = odd, sems, 0

    def make(self, dst, if_odd, if_even=None):
        sem = self.sems.at[self.taken]
        self.taken += 1
        return (dst, sem, if_odd, if_even)

    def start(self, load):
        dst, sem, if_odd, if_even = load
        if if_even is None:
            pltpu.make_async_copy(if_odd, dst, sem).start()
            return

        @pl.when(self.odd)
        def _():
            pltpu.make_async_copy(if_odd, dst, sem).start()

        @pl.when(jnp.logical_not(self.odd))
        def _():
            pltpu.make_async_copy(if_even, dst, sem).start()

    def wait(self, load):
        dst, sem, src, _ = load
        pltpu.make_async_copy(src, dst, sem).wait()


def chunk(ref, step, size):
    return ref.at[pl.ds(step * size, size), :]


def query_kernel(rows, heads, factor, odd_ref, a, b, x3, s3, g_hbm, h_hbm, near_hbm, q_hbm, gq_hbm, rq_hbm,
                 dq_hbm, w_hbm, stat_hbm, own, last, g_mem, h_mem, near_mem, q_mem, gain, scales, marks, tilt, dq_mem,
                 w_mem, stat_mem,
                 sems, out_sems):
    steps = heads // PER
    width = heads * HSIZE
    span = PER * rows
    odd = odd_ref[0] == 1
    loads = Loads(odd, sems)
    tail = 2 * heads * rows
    mark = pl.ds(tail, MARK_ROWS)
    small = [
        loads.make(marks.at[0], a.at[mark, :]),
        loads.make(marks.at[1], s3.at[mark, :], x3.at[mark, :]),
    ]
    later = [loads.make(scales, rq_hbm), loads.make(gain, gq_hbm), loads.make(q_mem, q_hbm)]
    blocks = [
        [
            loads.make(chunk(own, step, 2 * span), chunk(b, step, 2 * span), chunk(a, step, 2 * span)),
            loads.make(chunk(last, step, 2 * span), chunk(s3, step, 2 * span), chunk(x3, step, 2 * span)),
            loads.make(chunk(near_mem, step, span), chunk(near_hbm, step, span)),
        ]
        for step in range(steps)
    ]
    sums = [
        [
            loads.make(chunk(g_mem, step, span), chunk(g_hbm, step, span)),
            loads.make(chunk(h_mem, step, span), chunk(h_hbm, step, span)),
        ]
        for step in range(steps)
    ]
    for load in small + blocks[0] + sums[0] + later + blocks[1]:
        loads.start(load)
    for load in small:
        loads.wait(load)
    bias = jnp.where(mark_of(marks.at[0]) == mark_of(marks.at[1]), 0.0, NEG)
    lane = lax.broadcasted_iota(jnp.int32, (rows, HSIZE), 1)
    scale = 1.0 / math.sqrt(HSIZE)
    left = lane < HSIZE // 2
    lse = jnp.zeros((rows, HSIZE), F32)
    deltas = jnp.zeros((rows, HSIZE), F32)
    u_sum = jnp.zeros((rows, HSIZE), F32)
    w_rows = []
    for step in range(steps):
        for load in blocks[step]:
            loads.wait(load)
        if step + 1 < steps:
            for load in sums[step + 1] + (blocks[step + 2] if step + 2 < steps else []):
                loads.start(load)
        base = step * 2 * span
        keys, scores, dprobs = [], [], []
        for j in range(PER):
            top = slice(base + j * rows, base + (j + 1) * rows)
            low = slice(base + span + j * rows, base + span + (j + 1) * rows)
            keys.append(last[top, :])
            scores.append(dot_nt(own[top, :], keys[j]))
            dprobs.append(dot_nt(own[low, :], last[low, :]))
        fars, nears = [], []
        for j in range(PER):
            head = step * PER + j
            old = near_mem[head_rows(head, rows), :]
            turned = pltpu.roll(old, HSIZE // 2, 1)
            old_lse = jnp.where(left, old, turned)
            old_delta = jnp.where(left, turned, old)
            score = scores[j] * factor + bias
            best = jnp.maximum(old_lse, jnp.max(score, axis=-1, keepdims=True))
            prob = jnp.exp2(score - best)
            kept = jnp.exp2(old_lse - best)
            total = kept + jnp.sum(prob, axis=-1, keepdims=True)
            inverse = 1.0 / total
            kept = kept * inverse
            delta = kept * old_delta + jnp.sum(prob * dprobs[j], axis=-1, keepdims=True) * inverse
            fars.append(((prob * inverse) * (dprobs[j] - delta)).astype(BF16))
            nears.append((kept, old_delta - delta))
            lse = jnp.where(lane == head, best + jnp.log2(total), lse)
            deltas = jnp.where(lane == head, delta, deltas)
        if step == 0:
            for load in later:
                loads.wait(load)
            rq = scales[...]
        for load in sums[step]:
            loads.wait(load)
        for j in range(PER):
            head = step * PER + j
            out = head_rows(head, rows)
            cols = head_cols(head)
            kept, moved = nears[j]
            dq = (dot_nn(fars[j], keys[j]) + kept * (g_mem[out, :] + moved * h_mem[out, :])) * scale
            raw = q_mem[:, cols].astype(F32)
            tilted = dq * gain[head : head + 1, :]
            tilt[:, cols] = tilted
            u_sum = u_sum + raw * tilted
            w_rows.append(jnp.sum(dq * (raw * rq), axis=0, keepdims=True))
    stat_mem[:heads, :] = jnp.transpose(lse)[:heads, :]
    stat_mem[heads:, :] = jnp.transpose(deltas)[:heads, :]
    w_mem[...] = jnp.broadcast_to(jnp.concatenate(w_rows, axis=0).astype(BF16)[None], w_mem.shape)
    early = [
        pltpu.make_async_copy(stat_mem, stat_hbm, out_sems.at[steps]),
        pltpu.make_async_copy(w_mem, w_hbm, out_sems.at[steps + 1]),
    ]
    for copy in early:
        copy.start()
    low_part = rq * rq * rq * jnp.sum(u_sum, axis=-1, keepdims=True) * (1.0 / width)
    close_norm(heads, rq, low_part, tilt, q_mem, dq_mem, dq_hbm, out_sems)
    for copy in early:
        copy.wait()


def close_norm(heads, scale, low_part, tilt, raw, result, out_hbm, sems):
    steps = heads // PER
    size = PER * HSIZE
    copies = []
    for step in range(steps):
        for h in range(step * PER, (step + 1) * PER):
            cols = head_cols(h)
            result[:, cols] = (scale * tilt[:, cols] - raw[:, cols].astype(F32) * low_part).astype(BF16)
        some = pl.ds(step * size, size)
        copies.append(pltpu.make_async_copy(result.at[:, some], out_hbm.at[:, some], sems.at[step]))
        copies[-1].start()
    for copy in copies:
        copy.wait()


def key_kernel(rows, heads, factor, odd_ref, a, b, x1, s1, x2, s2, x3, s3, t0, t1, t2, t3, k_hbm, gk_hbm, rk_hbm,
               dk_hbm, dv_hbm, own, later, stats, k_mem, gain, scales, marks, tilt, dk_mem, dv_mem, sems, out_sems):
    steps = heads // PER
    width = heads * HSIZE
    span = PER * rows
    odd = odd_ref[0] == 1
    loads = Loads(odd, sems)
    mark = pl.ds(2 * heads * rows, MARK_ROWS)
    pairs = ((b, a), (x1, s1), (x2, s2), (x3, s3))
    small = [loads.make(stats.at[d], t) for d, t in enumerate((t0, t1, t2, t3))]
    small += [loads.make(marks.at[d], o.at[mark, :], e.at[mark, :]) for d, (o, e) in enumerate(pairs)]
    small += [loads.make(gain, gk_hbm)]
    last = [loads.make(scales, rk_hbm)]
    blocks = [
        [loads.make(chunk(own, step, 2 * span), chunk(a, step, 2 * span), chunk(b, step, 2 * span))]
        + [
            loads.make(chunk(later.at[d], step, 2 * span), chunk(o, step, 2 * span), chunk(e, step, 2 * span))
            for d, (o, e) in enumerate(pairs)
        ]
        for step in range(steps)
    ]
    whole_k = loads.make(k_mem, k_hbm)
    for load in small + blocks[0] + [whole_k] + blocks[1] + last:
        loads.start(load)
    for load in small:
        loads.wait(load)
    own_mark = mark_of(marks.at[0])
    bias = bias_row([jnp.where(mark_of(marks.at[d]) == own_mark, 0.0, NEG) for d in range(WIN)], rows)
    scale = 1.0 / math.sqrt(HSIZE)
    u_sum = jnp.zeros((rows, HSIZE), F32)
    copies = []
    for step in range(steps):
        for load in blocks[step] + ([whole_k] if step == 0 else []):
            loads.wait(load)
        if step + 2 < steps:
            for load in blocks[step + 2]:
                loads.start(load)
        base = step * 2 * span
        for j in range(PER):
            head = step * PER + j
            top = slice(base + j * rows, base + (j + 1) * rows)
            low = slice(base + span + j * rows, base + span + (j + 1) * rows)
            cols = head_cols(head)
            queries = jnp.concatenate([later[d, top, :] for d in range(WIN)], axis=0)
            d_outs = jnp.concatenate([later[d, low, :] for d in range(WIN)], axis=0)
            log_total = jnp.concatenate([stats[d, head : head + 1, :] for d in range(WIN)], axis=1)
            delta = jnp.concatenate([stats[d, heads + head : heads + head + 1, :] for d in range(WIN)], axis=1)
            probs = jnp.exp2(dot_nt(own[top, :], queries) * factor + (bias - log_total))
            dscores = probs * (dot_nt(own[low, :], d_outs) - delta)
            dv_mem[:, cols] = dot_nn(probs.astype(BF16), d_outs).astype(BF16)
            tilted = dot_nn(dscores.astype(BF16), queries) * (scale * gain[head : head + 1, :])
            tilt[:, cols] = tilted
            u_sum = u_sum + k_mem[:, cols].astype(F32) * tilted
        some = pl.ds(step * PER * HSIZE, PER * HSIZE)
        copies.append(pltpu.make_async_copy(dv_mem.at[:, some], dv_hbm.at[:, some], out_sems.at[steps + step]))
        copies[-1].start()
    loads.wait(last[0])
    rk = scales[...]
    low_part = rk * rk * rk * jnp.sum(u_sum, axis=-1, keepdims=True) * (1.0 / width)
    close_norm(heads, rk, low_part, tilt, k_mem, dk_mem, dk_hbm, out_sems)
    for copy in copies:
        copy.wait()


def spread_kernel(part_ref, one_ref, two_ref, three_ref, out_ref):
    del one_ref, two_ref, three_ref
    out_ref[...] = jnp.broadcast_to(jnp.sum(part_ref[...].astype(F32), axis=0).astype(BF16)[None], out_ref.shape)


def gains_kernel(part_ref, gq_ref, gk_ref, dq_ref, dk_ref):
    total = jnp.sum(part_ref[...].astype(F32), axis=0)
    dq_ref[...] = total
    dk_ref[...] = total * gq_ref[...] / gk_ref[...]


def params(limit=VMEM_LIMIT):
    return pltpu.CompilerParams(vmem_limit_bytes=limit)


def cost(flops, data=2**20):
    return pl.CostEstimate(flops=flops, bytes_accessed=data, transcendentals=0)


def shape(*dims, dtype=F32):
    return jax.ShapeDtypeStruct(dims, dtype)


def still(*dims):
    return pl.BlockSpec(dims, lambda i, odd: (0,) * len(dims))


def head_blocks(rows, used_if=None):
    def place(i, odd):
        if used_if is None:
            return (i, 0)
        return (i * odd[0] if used_if else i * (1 - odd[0]), 0)

    return pl.BlockSpec((PER * rows, HSIZE), place)


def body(q_in, k_in, v_in, gain_q, gain_k, d_out, video):
    rows, width = q_in.shape
    heads = width // HSIZE
    steps = heads // PER
    factor = math.log2(math.e) / math.sqrt(HSIZE)
    near_by, along = lax.axis_size("dp") * CORES, lax.axis_size("z")
    groups = near_by * along
    odd = lax.axis_index("core").astype(jnp.int32).reshape(1)
    gq = gain_q.reshape(heads, HSIZE)
    gk = gain_k.reshape(heads, HSIZE)
    packed_rows = 2 * heads * rows + MARK_ROWS
    pair_flops = 2 * rows * rows * HSIZE * heads
    smem = pl.BlockSpec(memory_space=pltpu.SMEM)
    vmem = pl.BlockSpec(memory_space=pltpu.VMEM)
    hbm = pl.BlockSpec(memory_space=pl.ANY)

    def gridded(kernel, name, flops, in_specs, out_specs, out_shape, scratch=(), limit=VMEM_LIMIT):
        return pl.pallas_call(
            kernel,
            grid_spec=pltpu.PrefetchScalarGridSpec(
                num_scalar_prefetch=1, grid=(steps,), in_specs=in_specs, out_specs=out_specs, scratch_shapes=scratch
            ),
            out_shape=out_shape,
            compiler_params=params(limit),
            cost_estimate=cost(flops),
            name=name,
        )

    packed = shape(packed_rows, HSIZE, dtype=BF16)
    a, b, rq, rk = pl.pallas_call(
        functools.partial(pack_kernel, heads),
        out_shape=(packed, packed, shape(rows, HSIZE), shape(rows, HSIZE)),
        in_specs=[smem, smem] + [hbm] * 6,
        out_specs=(hbm,) * 4,
        scratch_shapes=[
            pltpu.VMEM((4, rows, width), BF16),
            pltpu.VMEM((4, heads * rows, HSIZE), BF16),
            pltpu.VMEM((2, heads, HSIZE), F32),
            pltpu.VMEM((MARK_ROWS, HSIZE), BF16),
            pltpu.VMEM((2, rows, HSIZE), F32),
            pltpu.SemaphoreType.DMA((4, SPLIT + 1)),
            pltpu.SemaphoreType.DMA((4, steps + 1)),
        ],
        compiler_params=params(),
        cost_estimate=cost(pair_flops),
        name="pack",
    )(odd, video, q_in, k_in, d_out, v_in, gq, gk)

    cross = [(i, i + 1) for i in range(1, groups - 1, 2)] + [(i, i - 1) for i in range(2, groups, 2)]
    chip = [(i, i ^ 1) for i in range(groups)]
    next_chip = [(i, i + 2) for i in range(0, groups - 2, 2)] + [(i, i - 2) for i in range(3, groups, 2)]
    x1 = lax.ppermute(a, AXES, cross)
    s1 = lax.ppermute(b, AXES, chip)
    x2 = lax.ppermute(s1, AXES, cross)
    x3 = lax.ppermute(x1, AXES, next_chip)
    s2 = lax.ppermute(x1, AXES, chip)
    s3 = lax.ppermute(x2, AXES, chip)

    both = head_blocks(2 * rows)
    if_odd = head_blocks(2 * rows, True)
    if_even = head_blocks(2 * rows, False)
    tall = head_blocks(rows)
    mark = pl.BlockSpec((MARK_ROWS, HSIZE), lambda i, odd: (2 * heads * rows // MARK_ROWS, 0))
    cols = pl.BlockSpec((rows, PER * HSIZE), lambda i, odd: (0, i))
    square = still(rows, HSIZE)
    whole = still(rows, width)
    near = gridded(
        functools.partial(near_kernel, rows, factor), "near", 1024,
        [both, both, if_even, if_odd, if_even, if_odd] + [mark] * 5,
        (tall,) * 3,
        (shape(heads * rows, HSIZE),) * 3,
    )(odd, a, b, x1, s1, x2, s2, a, x1, s1, x2, s2)
    block = pltpu.VMEM((2 * heads * rows, HSIZE), BF16)
    flat = pltpu.VMEM((rows, width), BF16)
    wide = pltpu.VMEM((rows, width), F32)
    marks = lambda count: pltpu.VMEM((count, MARK_ROWS, HSIZE), BF16)
    gain_mem, scale_mem = pltpu.VMEM((heads, HSIZE), F32), pltpu.VMEM((rows, HSIZE), F32)
    sum_mem = pltpu.VMEM((heads * rows, HSIZE), F32)
    whole_shape = shape(rows, width, dtype=BF16)
    dq_in, w, stats = pl.pallas_call(
        functools.partial(query_kernel, rows, heads, factor),
        out_shape=(whole_shape, shape(along, heads, HSIZE, dtype=BF16), shape(2 * heads, rows)),
        in_specs=[smem] + [hbm] * 10,
        out_specs=(hbm,) * 3,
        scratch_shapes=[block, block, sum_mem, sum_mem, sum_mem, flat, gain_mem, scale_mem, marks(2), wide, flat,
                        pltpu.VMEM((along, heads, HSIZE), BF16), pltpu.VMEM((2 * heads, rows), F32),
                        pltpu.SemaphoreType.DMA((5 + 5 * steps,)), pltpu.SemaphoreType.DMA((steps + 2,))],
        compiler_params=params(),
        cost_estimate=cost(1024),
        name="query_side",
    )(odd, a, b, x3, s3, *near, q_in, gq, rq)

    def back(value, by):
        return lax.ppermute(value, AXES, [(i, i - by) for i in range(by, groups)])

    w = lax.all_to_all(w, "z", 0, 0)
    later = [back(stats, by) for by in range(1, WIN)]
    w = pl.pallas_call(
        spread_kernel,
        out_shape=shape(near_by, heads, HSIZE, dtype=BF16),
        in_specs=[vmem] + [hbm] * 3,
        out_specs=vmem,
        compiler_params=params(SMALL_LIMIT),
        cost_estimate=cost(2**20),
        name="spread",
    )(w, *later)
    w = lax.all_to_all(w, ("dp", "core"), 0, 0)
    dgain_q, dgain_k = pl.pallas_call(
        gains_kernel,
        out_shape=(shape(heads, HSIZE),) * 2,
        in_specs=[vmem] * 3,
        out_specs=(vmem,) * 2,
        compiler_params=params(SMALL_LIMIT),
        cost_estimate=cost(2**20),
        name="gains",
    )(w, gq, gk)

    dk_in, dv_in = pl.pallas_call(
        functools.partial(key_kernel, rows, heads, factor),
        out_shape=(whole_shape, whole_shape),
        in_specs=[smem] + [hbm] * 15,
        out_specs=(hbm, hbm),
        scratch_shapes=[block, pltpu.VMEM((WIN, 2 * heads * rows, HSIZE), BF16), pltpu.VMEM((WIN, 2 * heads, rows), F32),
                        flat, gain_mem, scale_mem, marks(WIN), wide, flat, flat,
                        pltpu.SemaphoreType.DMA((2 * WIN + 3 + (WIN + 1) * steps,)), pltpu.SemaphoreType.DMA((2 * steps,))],
        compiler_params=params(KEY_LIMIT),
        cost_estimate=cost(16 * pair_flops),
        name="key_side",
    )(odd, a, b, x1, s1, x2, s2, x3, s3, stats, *later, k_in, gk, rk)
    return dq_in, dk_in, dv_in, dgain_q.reshape(width), dgain_k.reshape(width)


def solution(mesh):
    dp, seq = mesh.devices.shape
    split = Mesh(mesh.devices.reshape(dp, seq // CORES, CORES), AXES)
    rows = P(AXES, None)
    return jax.shard_map(
        body,
        mesh=split,
        in_specs=(rows, rows, rows, P(), P(), rows, P(AXES)),
        out_specs=(rows, rows, rows, P(), P()),
        check_vma=False,
    )
```

```python
import functools
import math

import jax
import jax.numpy as jnp
from jax import lax
from jax.experimental import pallas as pl
from jax.experimental.pallas import tpu as pltpu
from jax.sharding import Mesh
from jax.sharding import PartitionSpec as P

HSIZE = 128
WIN = 4
EPS = 1e-06
NEG = -1e30
MARK_ROWS = 16
PER = 5
SPLIT = 4
AXES = ("dp", "z", "core")
CORES = 2
VMEM_LIMIT = 63 * 1024 * 1024
SMALL_LIMIT = 8 * 1024 * 1024
KEY_LIMIT = 62 * 1024 * 1024
F32 = jnp.float32
BF16 = jnp.bfloat16


def dot_nt(a, b):
    return lax.dot_general(a, b, (((1,), (1,)), ((), ())), preferred_element_type=F32)


def dot_nn(a, b):
    return lax.dot_general(a, b, (((1,), (0,)), ((), ())), preferred_element_type=F32)


def head_rows(j, rows):
    return slice(j * rows, (j + 1) * rows)


def head_cols(j):
    return slice(j * HSIZE, (j + 1) * HSIZE)


def pack_kernel(heads, odd_ref, video_ref, q_hbm, k_hbm, d_hbm, v_hbm, gq_hbm, gk_hbm,
                a_hbm, b_hbm, rq_hbm, rk_hbm, main, stage, gain, mark, scales, in_sems, out_sems):
    odd = odd_ref[0] == 1
    rows, width = q_hbm.shape
    size = rows // SPLIT
    steps = heads // PER
    span = PER * rows

    def load(which, src):
        return [
            pltpu.make_async_copy(
                src.at[pl.ds(part * size, size), :], main.at[which, pl.ds(part * size, size), :], in_sems.at[which, part]
            )
            for part in range(SPLIT)
        ]

    loads = [load(which, src) for which, src in enumerate((q_hbm, k_hbm, d_hbm, v_hbm))]
    gains = [
        pltpu.make_async_copy(src, gain.at[which], in_sems.at[which, SPLIT]) for which, src in enumerate((gq_hbm, gk_hbm))
    ]
    for copy in gains + loads[0] + loads[1] + loads[2] + loads[3]:
        copy.start()

    def store(which, step, dst):
        if step == steps:
            return pltpu.make_async_copy(
                mark, dst.at[pl.ds(2 * steps * span, MARK_ROWS), :], out_sems.at[which, steps]
            )
        return pltpu.make_async_copy(
            stage.at[which, pl.ds(step * span, span), :],
            dst.at[pl.ds((2 * step + which // 2) * span, span), :],
            out_sems.at[which, step],
        )

    def start_store(which, step):
        with_a = odd == (which % 2 == 1)

        @pl.when(with_a)
        def _():
            store(which, step, a_hbm).start()

        @pl.when(jnp.logical_not(with_a))
        def _():
            store(which, step, b_hbm).start()

    mark[...] = jnp.full((MARK_ROWS, HSIZE), (video_ref[0] + 1).astype(F32), F32).astype(BF16)
    for which in range(2):
        start_store(which, steps)
    for copy in gains:
        copy.wait()
    scale_stores = [
        pltpu.make_async_copy(scales.at[which], dst, out_sems.at[2 + which, steps])
        for which, dst in enumerate((rq_hbm, rk_hbm))
    ]
    for which in range(2):
        for copy in loads[which]:
            copy.wait()
        raw = main[which].astype(F32)
        scale = lax.rsqrt(jnp.sum(raw * raw, axis=-1, keepdims=True) * (1.0 / width) + EPS)
        scales[which] = jnp.broadcast_to(scale, (rows, HSIZE))
        scale_stores[which].start()
        for step in range(steps):
            for h in range(step * PER, (step + 1) * PER):
                normed = main[which, :, head_cols(h)].astype(F32) * scale * gain[which, h : h + 1, :]
                stage[which, head_rows(h, rows), :] = normed.astype(BF16)
            start_store(which, step)
    for which in (2, 3):
        for copy in loads[which]:
            copy.wait()
        for step in range(steps):
            for h in range(step * PER, (step + 1) * PER):
                stage[which, head_rows(h, rows), :] = main[which, :, head_cols(h)]
            start_store(which, step)
    for which in range(4):
        for step in range(steps + (which < 2)):
            store(which, step, a_hbm).wait()
    for copy in scale_stores:
        copy.wait()


def gate_kernel(*refs):
    del refs


def mark_of(ref):
    return ref[0:1, 0:1].astype(F32)


def bias_of(own_ref, odd, if_odd, if_even):
    mark = jnp.where(odd, mark_of(if_odd), mark_of(if_even))
    return jnp.where(mark == mark_of(own_ref), 0.0, NEG)


def bias_row(biases, rows):
    return jnp.concatenate([jnp.broadcast_to(bias, (1, rows)) for bias in biases], axis=1)


def softmax_part(best, score, dprob):
    prob = jnp.exp2(score - best)
    return prob, jnp.sum(prob, axis=-1, keepdims=True), jnp.sum(prob * dprob, axis=-1, keepdims=True)


def left_half(rows):
    return lax.broadcasted_iota(jnp.int32, (rows, HSIZE), 1) < HSIZE // 2


def halves(tile, left):
    turned = pltpu.roll(tile, HSIZE // 2, 1)
    return jnp.where(left, tile, turned), jnp.where(left, turned, tile)


def own_kernel(rows, factor, odd_ref, a, b, g_ref, h_ref, stat_ref):
    odd = odd_ref[0] == 1
    left = left_half(rows)
    keys, scores, dprobs = [], [], []
    for j in range(PER):
        top = head_rows(j, rows)
        low = head_rows(PER + j, rows)
        at, bt, al, bl = a[top, :], b[top, :], a[low, :], b[low, :]
        keys.append(jnp.where(odd, at, bt))
        scores.append(dot_nt(jnp.where(odd, bt, at), keys[j]))
        dprobs.append(dot_nt(jnp.where(odd, bl, al), jnp.where(odd, al, bl)))
    for j in range(PER):
        out = head_rows(j, rows)
        score = scores[j] * factor
        best = jnp.max(score, axis=-1, keepdims=True)
        prob, total, mixed = softmax_part(best, score, dprobs[j])
        inverse = 1.0 / total
        delta = mixed * inverse
        prob = prob * inverse
        both = jnp.concatenate([(prob * (dprobs[j] - delta)).astype(BF16), prob.astype(BF16)], axis=0)
        sums = dot_nn(both, keys[j])
        g_ref[out, :] = sums[:rows]
        h_ref[out, :] = sums[rows:]
        stat_ref[out, :] = jnp.where(left, best + jnp.log2(total), delta)


def near_kernel(rows, factor, odd_ref, a, b, x1, s1, x2, s2, am, x1m, s1m, x2m, s2m, g0, h0, stat0, g_ref, h_ref, stat_ref):
    odd = odd_ref[0] == 1
    bias = bias_row([bias_of(am, odd, s1m, x1m), bias_of(am, odd, s2m, x2m)], rows)
    pairs = ((s1, x1), (s2, x2))
    left = left_half(rows)
    keys, scores, dprobs = [], [], []
    for j in range(PER):
        top = head_rows(j, rows)
        low = head_rows(PER + j, rows)
        q = jnp.where(odd, b[top, :], a[top, :])
        d_out = jnp.where(odd, b[low, :], a[low, :])
        keys.append(jnp.concatenate([jnp.where(odd, o[top, :], e[top, :]) for o, e in pairs], axis=0))
        vals = jnp.concatenate([jnp.where(odd, o[low, :], e[low, :]) for o, e in pairs], axis=0)
        scores.append(dot_nt(q, keys[j]))
        dprobs.append(dot_nt(d_out, vals))
    for j in range(PER):
        out = head_rows(j, rows)
        old_lse, old_delta = halves(stat0[out, :], left)
        score = scores[j] * factor + bias
        best = jnp.maximum(old_lse, jnp.max(score, axis=-1, keepdims=True))
        kept = jnp.exp2(old_lse - best)
        prob, total, mixed = softmax_part(jnp.concatenate([best, best], axis=1), score, dprobs[j])
        total = kept + total
        inverse = 1.0 / total
        kept = kept * inverse
        delta = kept * old_delta + mixed * inverse
        inverse, change = [jnp.concatenate([value, value], axis=1) for value in (inverse, delta)]
        prob = prob * inverse
        both = jnp.concatenate([(prob * (dprobs[j] - change)).astype(BF16), prob.astype(BF16)], axis=0)
        sums = dot_nn(both, keys[j])
        g_ref[out, :] = sums[:rows] + kept * (g0[out, :] + (old_delta - delta) * h0[out, :])
        h_ref[out, :] = sums[rows:] + kept * h0[out, :]
        stat_ref[out, :] = jnp.where(left, best + jnp.log2(total), delta)


class Loads:
    def __init__(self, odd, sems):
        self.odd, self.sems, self.taken = odd, sems, 0

    def make(self, dst, if_odd, if_even=None):
        sem = self.sems.at[self.taken]
        self.taken += 1
        return (dst, sem, if_odd, if_even)

    def start(self, load):
        dst, sem, if_odd, if_even = load
        if if_even is None:
            pltpu.make_async_copy(if_odd, dst, sem).start()
            return

        @pl.when(self.odd)
        def _():
            pltpu.make_async_copy(if_odd, dst, sem).start()

        @pl.when(jnp.logical_not(self.odd))
        def _():
            pltpu.make_async_copy(if_even, dst, sem).start()

    def wait(self, load):
        dst, sem, src, _ = load
        pltpu.make_async_copy(src, dst, sem).wait()


def chunk(ref, step, size):
    return ref.at[pl.ds(step * size, size), :]


def query_kernel(rows, heads, factor, odd_ref, a, b, x3, s3, g_hbm, h_hbm, near_hbm, q_hbm, gq_hbm, rq_hbm,
                 dq_hbm, w_hbm, stat_hbm, own, last, g_mem, h_mem, near_mem, q_mem, gain, scales, marks, tilt, dq_mem,
                 w_mem, stat_mem,
                 sems, out_sems):
    steps = heads // PER
    width = heads * HSIZE
    span = PER * rows
    odd = odd_ref[0] == 1
    loads = Loads(odd, sems)
    tail = 2 * heads * rows
    mark = pl.ds(tail, MARK_ROWS)
    small = [
        loads.make(marks.at[0], a.at[mark, :]),
        loads.make(marks.at[1], s3.at[mark, :], x3.at[mark, :]),
    ]
    later = [loads.make(scales, rq_hbm), loads.make(gain, gq_hbm), loads.make(q_mem, q_hbm)]
    blocks = [
        [
            loads.make(chunk(own, step, 2 * span), chunk(b, step, 2 * span), chunk(a, step, 2 * span)),
            loads.make(chunk(last, step, 2 * span), chunk(s3, step, 2 * span), chunk(x3, step, 2 * span)),
            loads.make(chunk(near_mem, step, span), chunk(near_hbm, step, span)),
        ]
        for step in range(steps)
    ]
    sums = [
        [
            loads.make(chunk(g_mem, step, span), chunk(g_hbm, step, span)),
            loads.make(chunk(h_mem, step, span), chunk(h_hbm, step, span)),
        ]
        for step in range(steps)
    ]
    for load in small + blocks[0] + sums[0] + later + blocks[1]:
        loads.start(load)
    for load in small:
        loads.wait(load)
    bias = jnp.where(mark_of(marks.at[0]) == mark_of(marks.at[1]), 0.0, NEG)
    lane = lax.broadcasted_iota(jnp.int32, (rows, HSIZE), 1)
    scale = 1.0 / math.sqrt(HSIZE)
    left = lane < HSIZE // 2
    lse = jnp.zeros((rows, HSIZE), F32)
    deltas = jnp.zeros((rows, HSIZE), F32)
    u_sum = jnp.zeros((rows, HSIZE), F32)
    w_rows = []
    for step in range(steps):
        for load in blocks[step]:
            loads.wait(load)
        if step + 1 < steps:
            for load in sums[step + 1] + (blocks[step + 2] if step + 2 < steps else []):
                loads.start(load)
        base = step * 2 * span
        keys, scores, dprobs = [], [], []
        for j in range(PER):
            top = slice(base + j * rows, base + (j + 1) * rows)
            low = slice(base + span + j * rows, base + span + (j + 1) * rows)
            keys.append(last[top, :])
            scores.append(dot_nt(own[top, :], keys[j]))
            dprobs.append(dot_nt(own[low, :], last[low, :]))
        fars, nears = [], []
        for j in range(PER):
            head = step * PER + j
            old_lse, old_delta = halves(near_mem[head_rows(head, rows), :], left)
            score = scores[j] * factor + bias
            best = jnp.maximum(old_lse, jnp.max(score, axis=-1, keepdims=True))
            prob = jnp.exp2(score - best)
            kept = jnp.exp2(old_lse - best)
            total = kept + jnp.sum(prob, axis=-1, keepdims=True)
            inverse = 1.0 / total
            kept = kept * inverse
            delta = kept * old_delta + jnp.sum(prob * dprobs[j], axis=-1, keepdims=True) * inverse
            fars.append(((prob * inverse) * (dprobs[j] - delta)).astype(BF16))
            nears.append((kept, old_delta - delta))
            lse = jnp.where(lane == head, best + jnp.log2(total), lse)
            deltas = jnp.where(lane == head, delta, deltas)
        if step == 0:
            for load in later:
                loads.wait(load)
            rq = scales[...]
        for load in sums[step]:
            loads.wait(load)
        for j in range(PER):
            head = step * PER + j
            out = head_rows(head, rows)
            cols = head_cols(head)
            kept, moved = nears[j]
            dq = (dot_nn(fars[j], keys[j]) + kept * (g_mem[out, :] + moved * h_mem[out, :])) * scale
            raw = q_mem[:, cols].astype(F32)
            tilted = dq * gain[head : head + 1, :]
            tilt[:, cols] = tilted
            u_sum = u_sum + raw * tilted
            w_rows.append(jnp.sum(dq * (raw * rq), axis=0, keepdims=True))
    stat_mem[:heads, :] = jnp.transpose(lse)[:heads, :]
    stat_mem[heads:, :] = jnp.transpose(deltas)[:heads, :]
    w_mem[...] = jnp.broadcast_to(jnp.concatenate(w_rows, axis=0).astype(BF16)[None], w_mem.shape)
    early = [
        pltpu.make_async_copy(stat_mem, stat_hbm, out_sems.at[steps]),
        pltpu.make_async_copy(w_mem, w_hbm, out_sems.at[steps + 1]),
    ]
    for copy in early:
        copy.start()
    low_part = rq * rq * rq * jnp.sum(u_sum, axis=-1, keepdims=True) * (1.0 / width)
    close_norm(heads, rq, low_part, tilt, q_mem, dq_mem, dq_hbm, out_sems)
    for copy in early:
        copy.wait()


def close_norm(heads, scale, low_part, tilt, raw, result, out_hbm, sems):
    steps = heads // PER
    size = PER * HSIZE
    copies = []
    for step in range(steps):
        for h in range(step * PER, (step + 1) * PER):
            cols = head_cols(h)
            result[:, cols] = (scale * tilt[:, cols] - raw[:, cols].astype(F32) * low_part).astype(BF16)
        some = pl.ds(step * size, size)
        copies.append(pltpu.make_async_copy(result.at[:, some], out_hbm.at[:, some], sems.at[step]))
        copies[-1].start()
    for copy in copies:
        copy.wait()


def key_kernel(rows, heads, factor, odd_ref, a, b, x1, s1, x2, s2, x3, s3, t0, t1, t2, t3, k_hbm, gk_hbm, rk_hbm,
               dk_hbm, dv_hbm, own, later, stats, k_mem, gain, scales, marks, tilt, dk_mem, dv_mem, sems, out_sems):
    steps = heads // PER
    width = heads * HSIZE
    span = PER * rows
    odd = odd_ref[0] == 1
    loads = Loads(odd, sems)
    mark = pl.ds(2 * heads * rows, MARK_ROWS)
    pairs = ((b, a), (x1, s1), (x2, s2), (x3, s3))
    small = [loads.make(stats.at[d], t) for d, t in enumerate((t0, t1, t2, t3))]
    small += [loads.make(marks.at[d], o.at[mark, :], e.at[mark, :]) for d, (o, e) in enumerate(pairs)]
    small += [loads.make(gain, gk_hbm)]
    last = [loads.make(scales, rk_hbm)]
    blocks = [
        [loads.make(chunk(own, step, 2 * span), chunk(a, step, 2 * span), chunk(b, step, 2 * span))]
        + [
            loads.make(chunk(later.at[d], step, 2 * span), chunk(o, step, 2 * span), chunk(e, step, 2 * span))
            for d, (o, e) in enumerate(pairs)
        ]
        for step in range(steps)
    ]
    whole_k = loads.make(k_mem, k_hbm)
    for load in small + blocks[0] + [whole_k] + blocks[1] + last:
        loads.start(load)
    for load in small:
        loads.wait(load)
    own_mark = mark_of(marks.at[0])
    bias = bias_row([jnp.where(mark_of(marks.at[d]) == own_mark, 0.0, NEG) for d in range(WIN)], rows)
    scale = 1.0 / math.sqrt(HSIZE)
    u_sum = jnp.zeros((rows, HSIZE), F32)
    copies = []
    for step in range(steps):
        for load in blocks[step] + ([whole_k] if step == 0 else []):
            loads.wait(load)
        if step + 2 < steps:
            for load in blocks[step + 2]:
                loads.start(load)
        base = step * 2 * span
        for j in range(PER):
            head = step * PER + j
            top = slice(base + j * rows, base + (j + 1) * rows)
            low = slice(base + span + j * rows, base + span + (j + 1) * rows)
            cols = head_cols(head)
            queries = jnp.concatenate([later[d, top, :] for d in range(WIN)], axis=0)
            d_outs = jnp.concatenate([later[d, low, :] for d in range(WIN)], axis=0)
            log_total = jnp.concatenate([stats[d, head : head + 1, :] for d in range(WIN)], axis=1)
            delta = jnp.concatenate([stats[d, heads + head : heads + head + 1, :] for d in range(WIN)], axis=1)
            probs = jnp.exp2(dot_nt(own[top, :], queries) * factor + (bias - log_total))
            dscores = probs * (dot_nt(own[low, :], d_outs) - delta)
            dv_mem[:, cols] = dot_nn(probs.astype(BF16), d_outs).astype(BF16)
            tilted = dot_nn(dscores.astype(BF16), queries) * (scale * gain[head : head + 1, :])
            tilt[:, cols] = tilted
            u_sum = u_sum + k_mem[:, cols].astype(F32) * tilted
        some = pl.ds(step * PER * HSIZE, PER * HSIZE)
        copies.append(pltpu.make_async_copy(dv_mem.at[:, some], dv_hbm.at[:, some], out_sems.at[steps + step]))
        copies[-1].start()
    loads.wait(last[0])
    rk = scales[...]
    low_part = rk * rk * rk * jnp.sum(u_sum, axis=-1, keepdims=True) * (1.0 / width)
    close_norm(heads, rk, low_part, tilt, k_mem, dk_mem, dk_hbm, out_sems)
    for copy in copies:
        copy.wait()


def spread_kernel(part_ref, one_ref, two_ref, three_ref, out_ref):
    del one_ref, two_ref, three_ref
    out_ref[...] = jnp.broadcast_to(jnp.sum(part_ref[...].astype(F32), axis=0).astype(BF16)[None], out_ref.shape)


def gains_kernel(part_ref, gq_ref, gk_ref, dq_ref, dk_ref):
    total = jnp.sum(part_ref[...].astype(F32), axis=0)
    dq_ref[...] = total
    dk_ref[...] = total * gq_ref[...] / gk_ref[...]


def params(limit=VMEM_LIMIT):
    return pltpu.CompilerParams(vmem_limit_bytes=limit)


def cost(flops, data=2**20):
    return pl.CostEstimate(flops=flops, bytes_accessed=data, transcendentals=0)


def shape(*dims, dtype=F32):
    return jax.ShapeDtypeStruct(dims, dtype)


def still(*dims):
    return pl.BlockSpec(dims, lambda i, odd: (0,) * len(dims))


def head_blocks(rows, used_if=None):
    def place(i, odd):
        if used_if is None:
            return (i, 0)
        return (i * odd[0] if used_if else i * (1 - odd[0]), 0)

    return pl.BlockSpec((PER * rows, HSIZE), place)


def body(q_in, k_in, v_in, gain_q, gain_k, d_out, video):
    rows, width = q_in.shape
    heads = width // HSIZE
    steps = heads // PER
    factor = math.log2(math.e) / math.sqrt(HSIZE)
    near_by, along = lax.axis_size("dp") * CORES, lax.axis_size("z")
    groups = near_by * along
    odd = lax.axis_index("core").astype(jnp.int32).reshape(1)
    gq = gain_q.reshape(heads, HSIZE)
    gk = gain_k.reshape(heads, HSIZE)
    packed_rows = 2 * heads * rows + MARK_ROWS
    pair_flops = 2 * rows * rows * HSIZE * heads
    smem = pl.BlockSpec(memory_space=pltpu.SMEM)
    vmem = pl.BlockSpec(memory_space=pltpu.VMEM)
    hbm = pl.BlockSpec(memory_space=pl.ANY)

    def after(value, flops, *others):
        return pl.pallas_call(
            gate_kernel,
            out_shape=jax.ShapeDtypeStruct(value.shape, value.dtype),
            in_specs=[hbm] * (1 + len(others)),
            out_specs=hbm,
            input_output_aliases={0: 0},
            compiler_params=params(),
            cost_estimate=cost(flops),
            name="gate",
        )(value, *others)

    def gridded(kernel, name, flops, in_specs, out_specs, out_shape, scratch=(), limit=VMEM_LIMIT):
        return pl.pallas_call(
            kernel,
            grid_spec=pltpu.PrefetchScalarGridSpec(
                num_scalar_prefetch=1, grid=(steps,), in_specs=in_specs, out_specs=out_specs, scratch_shapes=scratch
            ),
            out_shape=out_shape,
            compiler_params=params(limit),
            cost_estimate=cost(flops),
            name=name,
        )

    packed = shape(packed_rows, HSIZE, dtype=BF16)
    a, b, rq, rk = pl.pallas_call(
        functools.partial(pack_kernel, heads),
        out_shape=(packed, packed, shape(rows, HSIZE), shape(rows, HSIZE)),
        in_specs=[smem, smem] + [hbm] * 6,
        out_specs=(hbm,) * 4,
        scratch_shapes=[
            pltpu.VMEM((4, rows, width), BF16),
            pltpu.VMEM((4, heads * rows, HSIZE), BF16),
            pltpu.VMEM((2, heads, HSIZE), F32),
            pltpu.VMEM((MARK_ROWS, HSIZE), BF16),
            pltpu.VMEM((2, rows, HSIZE), F32),
            pltpu.SemaphoreType.DMA((4, SPLIT + 1)),
            pltpu.SemaphoreType.DMA((4, steps + 1)),
        ],
        compiler_params=params(),
        cost_estimate=cost(pair_flops),
        name="pack",
    )(odd, video, q_in, k_in, d_out, v_in, gq, gk)

    cross = [(i, i + 1) for i in range(1, groups - 1, 2)] + [(i, i - 1) for i in range(2, groups, 2)]
    chip = [(i, i ^ 1) for i in range(groups)]
    next_chip = [(i, i + 2) for i in range(0, groups - 2, 2)] + [(i, i - 2) for i in range(3, groups, 2)]
    both = head_blocks(2 * rows)
    if_odd = head_blocks(2 * rows, True)
    if_even = head_blocks(2 * rows, False)
    tall = head_blocks(rows)
    mark = pl.BlockSpec((MARK_ROWS, HSIZE), lambda i, odd: (2 * heads * rows // MARK_ROWS, 0))
    cols = pl.BlockSpec((rows, PER * HSIZE), lambda i, odd: (0, i))
    square = still(rows, HSIZE)
    whole = still(rows, width)
    sums_shape = (shape(heads * rows, HSIZE),) * 3
    x1 = after(lax.ppermute(a, AXES, cross), 2 * pair_flops)
    sums = gridded(
        functools.partial(own_kernel, rows, factor), "own", 1024, [both, both], (tall,) * 3, sums_shape
    )(odd, a, b)
    b = after(b, 0, sums[2])
    x2 = lax.ppermute(b, AXES, next_chip)
    x3 = after(lax.ppermute(x1, AXES, next_chip), pair_flops)
    s1 = lax.ppermute(b, AXES, chip)
    s2 = lax.ppermute(x1, AXES, chip)
    s3 = lax.ppermute(x2, AXES, chip)

    near = gridded(
        functools.partial(near_kernel, rows, factor), "near", 1024,
        [if_even, if_odd, if_even, if_odd, if_even, if_odd] + [mark] * 5 + [tall] * 3,
        (tall,) * 3,
        sums_shape,
    )(odd, a, b, x1, s1, x2, s2, a, x1, s1, x2, s2, *sums)
    block = pltpu.VMEM((2 * heads * rows, HSIZE), BF16)
    flat = pltpu.VMEM((rows, width), BF16)
    wide = pltpu.VMEM((rows, width), F32)
    marks = lambda count: pltpu.VMEM((count, MARK_ROWS, HSIZE), BF16)
    gain_mem, scale_mem = pltpu.VMEM((heads, HSIZE), F32), pltpu.VMEM((rows, HSIZE), F32)
    sum_mem = pltpu.VMEM((heads * rows, HSIZE), F32)
    whole_shape = shape(rows, width, dtype=BF16)
    dq_in, w, stats = pl.pallas_call(
        functools.partial(query_kernel, rows, heads, factor),
        out_shape=(whole_shape, shape(along, heads, HSIZE, dtype=BF16), shape(2 * heads, rows)),
        in_specs=[smem] + [hbm] * 10,
        out_specs=(hbm,) * 3,
        scratch_shapes=[block, block, sum_mem, sum_mem, sum_mem, flat, gain_mem, scale_mem, marks(2), wide, flat,
                        pltpu.VMEM((along, heads, HSIZE), BF16), pltpu.VMEM((2 * heads, rows), F32),
                        pltpu.SemaphoreType.DMA((5 + 5 * steps,)), pltpu.SemaphoreType.DMA((steps + 2,))],
        compiler_params=params(),
        cost_estimate=cost(1024),
        name="query_side",
    )(odd, a, b, x3, s3, *near, q_in, gq, rq)

    def back(value, by):
        return lax.ppermute(value, AXES, [(i, i - by) for i in range(by, groups)])

    w = lax.all_to_all(w, "z", 0, 0)
    later = [back(stats, by) for by in range(1, WIN)]
    w = pl.pallas_call(
        spread_kernel,
        out_shape=shape(near_by, heads, HSIZE, dtype=BF16),
        in_specs=[vmem] + [hbm] * 3,
        out_specs=vmem,
        compiler_params=params(SMALL_LIMIT),
        cost_estimate=cost(2**20),
        name="spread",
    )(w, *later)
    w = lax.all_to_all(w, ("dp", "core"), 0, 0)
    dgain_q, dgain_k = pl.pallas_call(
        gains_kernel,
        out_shape=(shape(heads, HSIZE),) * 2,
        in_specs=[vmem] * 3,
        out_specs=(vmem,) * 2,
        compiler_params=params(SMALL_LIMIT),
        cost_estimate=cost(2**20),
        name="gains",
    )(w, gq, gk)

    dk_in, dv_in = pl.pallas_call(
        functools.partial(key_kernel, rows, heads, factor),
        out_shape=(whole_shape, whole_shape),
        in_specs=[smem] + [hbm] * 15,
        out_specs=(hbm, hbm),
        scratch_shapes=[block, pltpu.VMEM((WIN, 2 * heads * rows, HSIZE), BF16), pltpu.VMEM((WIN, 2 * heads, rows), F32),
                        flat, gain_mem, scale_mem, marks(WIN), wide, flat, flat,
                        pltpu.SemaphoreType.DMA((2 * WIN + 3 + (WIN + 1) * steps,)), pltpu.SemaphoreType.DMA((2 * steps,))],
        compiler_params=params(KEY_LIMIT),
        cost_estimate=cost(16 * pair_flops),
        name="key_side",
    )(odd, a, b, x1, s1, x2, s2, x3, s3, stats, *later, k_in, gk, rk)
    return dq_in, dk_in, dv_in, dgain_q.reshape(width), dgain_k.reshape(width)


def solution(mesh):
    dp, seq = mesh.devices.shape
    split = Mesh(mesh.devices.reshape(dp, seq // CORES, CORES), AXES)
    rows = P(AXES, None)
    return jax.shard_map(
        body,
        mesh=split,
        in_specs=(rows, rows, rows, P(), P(), rows, P(AXES)),
        out_specs=(rows, rows, rows, P(), P()),
        check_vma=False,
    )
```

```python
import functools
import math

import jax
import jax.numpy as jnp
from jax import lax
from jax.experimental import pallas as pl
from jax.experimental.pallas import tpu as pltpu
from jax.sharding import Mesh
from jax.sharding import PartitionSpec as P

HSIZE = 128
WIN = 4
EPS = 1e-06
NEG = -1e30
MARK_ROWS = 16
PER = 5
SPLIT = 4
AXES = ("dp", "z", "core")
CORES = 2
VMEM_LIMIT = 63 * 1024 * 1024
SMALL_LIMIT = 8 * 1024 * 1024
KEY_LIMIT = 62 * 1024 * 1024
F32 = jnp.float32
BF16 = jnp.bfloat16


def dot_nt(a, b):
    return lax.dot_general(a, b, (((1,), (1,)), ((), ())), preferred_element_type=F32)


def dot_nn(a, b):
    return lax.dot_general(a, b, (((1,), (0,)), ((), ())), preferred_element_type=F32)


def head_rows(j, rows):
    return slice(j * rows, (j + 1) * rows)


def head_cols(j):
    return slice(j * HSIZE, (j + 1) * HSIZE)


def pack_kernel(heads, odd_ref, video_ref, q_hbm, k_hbm, d_hbm, v_hbm, gq_hbm, gk_hbm,
                a_hbm, b_hbm, rq_hbm, rk_hbm, main, stage, gain, mark, scales, in_sems, out_sems):
    odd = odd_ref[0] == 1
    rows, width = q_hbm.shape
    size = rows // SPLIT
    steps = heads // PER
    span = PER * rows

    def load(which, src):
        return [
            pltpu.make_async_copy(
                src.at[pl.ds(part * size, size), :], main.at[which, pl.ds(part * size, size), :], in_sems.at[which, part]
            )
            for part in range(SPLIT)
        ]

    loads = [load(which, src) for which, src in enumerate((q_hbm, k_hbm, d_hbm, v_hbm))]
    gains = [
        pltpu.make_async_copy(src, gain.at[which], in_sems.at[which, SPLIT]) for which, src in enumerate((gq_hbm, gk_hbm))
    ]
    for copy in gains + loads[0] + loads[1] + loads[2] + loads[3]:
        copy.start()

    def store(which, step, dst):
        if step == steps:
            return pltpu.make_async_copy(
                mark, dst.at[pl.ds(2 * steps * span, MARK_ROWS), :], out_sems.at[which, steps]
            )
        return pltpu.make_async_copy(
            stage.at[which, pl.ds(step * span, span), :],
            dst.at[pl.ds((2 * step + which // 2) * span, span), :],
            out_sems.at[which, step],
        )

    def start_store(which, step):
        with_a = odd == (which % 2 == 1)

        @pl.when(with_a)
        def _():
            store(which, step, a_hbm).start()

        @pl.when(jnp.logical_not(with_a))
        def _():
            store(which, step, b_hbm).start()

    mark[...] = jnp.full((MARK_ROWS, HSIZE), (video_ref[0] + 1).astype(F32), F32).astype(BF16)
    for which in range(2):
        start_store(which, steps)
    for copy in gains:
        copy.wait()
    scale_stores = [
        pltpu.make_async_copy(scales.at[which], dst, out_sems.at[2 + which, steps])
        for which, dst in enumerate((rq_hbm, rk_hbm))
    ]
    for which in range(2):
        for copy in loads[which]:
            copy.wait()
        raw = main[which].astype(F32)
        scale = lax.rsqrt(jnp.sum(raw * raw, axis=-1, keepdims=True) * (1.0 / width) + EPS)
        scales[which] = jnp.broadcast_to(scale, (rows, HSIZE))
        scale_stores[which].start()
        for step in range(steps):
            for h in range(step * PER, (step + 1) * PER):
                normed = main[which, :, head_cols(h)].astype(F32) * scale * gain[which, h : h + 1, :]
                stage[which, head_rows(h, rows), :] = normed.astype(BF16)
            start_store(which, step)
    for which in (2, 3):
        for copy in loads[which]:
            copy.wait()
        for step in range(steps):
            for h in range(step * PER, (step + 1) * PER):
                stage[which, head_rows(h, rows), :] = main[which, :, head_cols(h)]
            start_store(which, step)
    for which in range(4):
        for step in range(steps + (which < 2)):
            store(which, step, a_hbm).wait()
    for copy in scale_stores:
        copy.wait()


def gate_kernel(*refs):
    del refs


def mark_of(ref):
    return ref[0:1, 0:1].astype(F32)


def bias_of(own_ref, odd, if_odd, if_even):
    mark = jnp.where(odd, mark_of(if_odd), mark_of(if_even))
    return jnp.where(mark == mark_of(own_ref), 0.0, NEG)


def bias_row(biases, rows):
    return jnp.concatenate([jnp.broadcast_to(bias, (1, rows)) for bias in biases], axis=1)


def softmax_part(best, score, dprob):
    prob = jnp.exp2(score - best)
    return prob, jnp.sum(prob, axis=-1, keepdims=True), jnp.sum(prob * dprob, axis=-1, keepdims=True)


def left_half(rows):
    return lax.broadcasted_iota(jnp.int32, (rows, HSIZE), 1) < HSIZE // 2


def halves(tile, left):
    turned = pltpu.roll(tile, HSIZE // 2, 1)
    return jnp.where(left, tile, turned), jnp.where(left, turned, tile)


def own_kernel(rows, factor, odd_ref, a, b, g_ref, h_ref, stat_ref):
    odd = odd_ref[0] == 1
    left = left_half(rows)
    keys, scores, dprobs = [], [], []
    for j in range(PER):
        top = head_rows(j, rows)
        low = head_rows(PER + j, rows)
        at, bt, al, bl = a[top, :], b[top, :], a[low, :], b[low, :]
        keys.append(jnp.where(odd, at, bt))
        scores.append(dot_nt(jnp.where(odd, bt, at), keys[j]))
        dprobs.append(dot_nt(jnp.where(odd, bl, al), jnp.where(odd, al, bl)))
    for j in range(PER):
        out = head_rows(j, rows)
        score = scores[j] * factor
        best = jnp.max(score, axis=-1, keepdims=True)
        prob, total, mixed = softmax_part(best, score, dprobs[j])
        inverse = 1.0 / total
        delta = mixed * inverse
        prob = prob * inverse
        both = jnp.concatenate([(prob * (dprobs[j] - delta)).astype(BF16), prob.astype(BF16)], axis=0)
        sums = dot_nn(both, keys[j])
        g_ref[out, :] = sums[:rows]
        h_ref[out, :] = sums[rows:]
        stat_ref[out, :] = jnp.where(left, best + jnp.log2(total), delta)


def near_kernel(rows, factor, odd_ref, a, b, x1, s1, am, x1m, s1m, g0, h0, stat0, g_ref, h_ref, stat_ref):
    odd = odd_ref[0] == 1
    bias = bias_of(am, odd, s1m, x1m)
    left = left_half(rows)
    keys, scores, dprobs = [], [], []
    for j in range(PER):
        top = head_rows(j, rows)
        low = head_rows(PER + j, rows)
        q = jnp.where(odd, b[top, :], a[top, :])
        d_out = jnp.where(odd, b[low, :], a[low, :])
        keys.append(jnp.where(odd, s1[top, :], x1[top, :]))
        vals = jnp.where(odd, s1[low, :], x1[low, :])
        scores.append(dot_nt(q, keys[j]))
        dprobs.append(dot_nt(d_out, vals))
    for j in range(PER):
        out = head_rows(j, rows)
        old_lse, old_delta = halves(stat0[out, :], left)
        score = scores[j] * factor + bias
        best = jnp.maximum(old_lse, jnp.max(score, axis=-1, keepdims=True))
        kept = jnp.exp2(old_lse - best)
        prob, total, mixed = softmax_part(best, score, dprobs[j])
        total = kept + total
        inverse = 1.0 / total
        kept = kept * inverse
        delta = kept * old_delta + mixed * inverse
        prob = prob * inverse
        both = jnp.concatenate([(prob * (dprobs[j] - delta)).astype(BF16), prob.astype(BF16)], axis=0)
        sums = dot_nn(both, keys[j])
        g_ref[out, :] = sums[:rows] + kept * (g0[out, :] + (old_delta - delta) * h0[out, :])
        h_ref[out, :] = sums[rows:] + kept * h0[out, :]
        stat_ref[out, :] = jnp.where(left, best + jnp.log2(total), delta)


class Loads:
    def __init__(self, odd, sems):
        self.odd, self.sems, self.taken = odd, sems, 0

    def make(self, dst, if_odd, if_even=None):
        sem = self.sems.at[self.taken]
        self.taken += 1
        return (dst, sem, if_odd, if_even)

    def start(self, load):
        dst, sem, if_odd, if_even = load
        if if_even is None:
            pltpu.make_async_copy(if_odd, dst, sem).start()
            return

        @pl.when(self.odd)
        def _():
            pltpu.make_async_copy(if_odd, dst, sem).start()

        @pl.when(jnp.logical_not(self.odd))
        def _():
            pltpu.make_async_copy(if_even, dst, sem).start()

    def wait(self, load):
        dst, sem, src, _ = load
        pltpu.make_async_copy(src, dst, sem).wait()


def chunk(ref, step, size):
    return ref.at[pl.ds(step * size, size), :]


def query_kernel(rows, heads, factor, odd_ref, a, b, x2, s2, x3, s3, g_hbm, h_hbm, near_hbm, q_hbm, gq_hbm, rq_hbm,
                 dq_hbm, w_hbm, stat_hbm, own, last, g_mem, h_mem, near_mem, q_mem, gain, scales, marks, tilt, dq_mem,
                 w_mem, stat_mem,
                 sems, out_sems):
    steps = heads // PER
    width = heads * HSIZE
    span = PER * rows
    odd = odd_ref[0] == 1
    loads = Loads(odd, sems)
    tail = 2 * heads * rows
    mark = pl.ds(tail, MARK_ROWS)
    small = [
        loads.make(marks.at[0], a.at[mark, :]),
        loads.make(marks.at[1], s2.at[mark, :], x2.at[mark, :]),
        loads.make(marks.at[2], s3.at[mark, :], x3.at[mark, :]),
    ]
    later = [loads.make(scales, rq_hbm), loads.make(gain, gq_hbm), loads.make(q_mem, q_hbm)]
    blocks = [
        [
            loads.make(chunk(own, step, 2 * span), chunk(b, step, 2 * span), chunk(a, step, 2 * span)),
            loads.make(chunk(last.at[0], step, 2 * span), chunk(s2, step, 2 * span), chunk(x2, step, 2 * span)),
            loads.make(chunk(last.at[1], step, 2 * span), chunk(s3, step, 2 * span), chunk(x3, step, 2 * span)),
            loads.make(chunk(near_mem, step, span), chunk(near_hbm, step, span)),
        ]
        for step in range(steps)
    ]
    sums = [
        [
            loads.make(chunk(g_mem, step, span), chunk(g_hbm, step, span)),
            loads.make(chunk(h_mem, step, span), chunk(h_hbm, step, span)),
        ]
        for step in range(steps)
    ]
    for load in small + blocks[0] + sums[0] + later + blocks[1]:
        loads.start(load)
    for load in small:
        loads.wait(load)
    bias = bias_row([jnp.where(mark_of(marks.at[0]) == mark_of(marks.at[d]), 0.0, NEG) for d in (1, 2)], rows)
    lane = lax.broadcasted_iota(jnp.int32, (rows, HSIZE), 1)
    scale = 1.0 / math.sqrt(HSIZE)
    left = lane < HSIZE // 2
    lse = jnp.zeros((rows, HSIZE), F32)
    deltas = jnp.zeros((rows, HSIZE), F32)
    u_sum = jnp.zeros((rows, HSIZE), F32)
    w_rows = []
    for step in range(steps):
        for load in blocks[step]:
            loads.wait(load)
        if step + 1 < steps:
            for load in sums[step + 1] + (blocks[step + 2] if step + 2 < steps else []):
                loads.start(load)
        base = step * 2 * span
        keys, scores, dprobs = [], [], []
        for j in range(PER):
            top = slice(base + j * rows, base + (j + 1) * rows)
            low = slice(base + span + j * rows, base + span + (j + 1) * rows)
            keys.append(jnp.concatenate([last[0, top, :], last[1, top, :]], axis=0))
            scores.append(dot_nt(own[top, :], keys[j]))
            dprobs.append(dot_nt(own[low, :], jnp.concatenate([last[0, low, :], last[1, low, :]], axis=0)))
        fars, nears = [], []
        for j in range(PER):
            head = step * PER + j
            old_lse, old_delta = halves(near_mem[head_rows(head, rows), :], left)
            score = scores[j] * factor + bias
            best = jnp.maximum(old_lse, jnp.max(score, axis=-1, keepdims=True))
            kept = jnp.exp2(old_lse - best)
            prob, total, mixed = softmax_part(jnp.concatenate([best, best], axis=1), score, dprobs[j])
            total = kept + total
            inverse = 1.0 / total
            kept = kept * inverse
            delta = kept * old_delta + mixed * inverse
            both = [jnp.concatenate([value, value], axis=1) for value in (inverse, delta)]
            fars.append(((prob * both[0]) * (dprobs[j] - both[1])).astype(BF16))
            nears.append((kept, old_delta - delta))
            lse = jnp.where(lane == head, best + jnp.log2(total), lse)
            deltas = jnp.where(lane == head, delta, deltas)
        if step == 0:
            for load in later:
                loads.wait(load)
            rq = scales[...]
        for load in sums[step]:
            loads.wait(load)
        for j in range(PER):
            head = step * PER + j
            out = head_rows(head, rows)
            cols = head_cols(head)
            kept, moved = nears[j]
            dq = (dot_nn(fars[j], keys[j]) + kept * (g_mem[out, :] + moved * h_mem[out, :])) * scale
            raw = q_mem[:, cols].astype(F32)
            tilted = dq * gain[head : head + 1, :]
            tilt[:, cols] = tilted
            u_sum = u_sum + raw * tilted
            w_rows.append(jnp.sum(dq * (raw * rq), axis=0, keepdims=True))
    stat_mem[:heads, :] = jnp.transpose(lse)[:heads, :]
    stat_mem[heads:, :] = jnp.transpose(deltas)[:heads, :]
    w_mem[...] = jnp.broadcast_to(jnp.concatenate(w_rows, axis=0).astype(BF16)[None], w_mem.shape)
    early = [
        pltpu.make_async_copy(stat_mem, stat_hbm, out_sems.at[steps]),
        pltpu.make_async_copy(w_mem, w_hbm, out_sems.at[steps + 1]),
    ]
    for copy in early:
        copy.start()
    low_part = rq * rq * rq * jnp.sum(u_sum, axis=-1, keepdims=True) * (1.0 / width)
    close_norm(heads, rq, low_part, tilt, q_mem, dq_mem, dq_hbm, out_sems)
    for copy in early:
        copy.wait()


def close_norm(heads, scale, low_part, tilt, raw, result, out_hbm, sems):
    steps = heads // PER
    size = PER * HSIZE
    copies = []
    for step in range(steps):
        for h in range(step * PER, (step + 1) * PER):
            cols = head_cols(h)
            result[:, cols] = (scale * tilt[:, cols] - raw[:, cols].astype(F32) * low_part).astype(BF16)
        some = pl.ds(step * size, size)
        copies.append(pltpu.make_async_copy(result.at[:, some], out_hbm.at[:, some], sems.at[step]))
        copies[-1].start()
    for copy in copies:
        copy.wait()


def key_kernel(rows, heads, factor, odd_ref, a, b, x1, s1, x2, s2, x3, s3, t0, t1, t2, t3, k_hbm, gk_hbm, rk_hbm,
               dk_hbm, dv_hbm, own, later, stats, k_mem, gain, scales, marks, tilt, dk_mem, dv_mem, sems, out_sems):
    steps = heads // PER
    width = heads * HSIZE
    span = PER * rows
    odd = odd_ref[0] == 1
    loads = Loads(odd, sems)
    mark = pl.ds(2 * heads * rows, MARK_ROWS)
    pairs = ((b, a), (x1, s1), (x2, s2), (x3, s3))
    small = [loads.make(stats.at[d], t) for d, t in enumerate((t0, t1, t2, t3))]
    small += [loads.make(marks.at[d], o.at[mark, :], e.at[mark, :]) for d, (o, e) in enumerate(pairs)]
    small += [loads.make(gain, gk_hbm)]
    last = [loads.make(scales, rk_hbm)]
    blocks = [
        [loads.make(chunk(own, step, 2 * span), chunk(a, step, 2 * span), chunk(b, step, 2 * span))]
        + [
            loads.make(chunk(later.at[d], step, 2 * span), chunk(o, step, 2 * span), chunk(e, step, 2 * span))
            for d, (o, e) in enumerate(pairs)
        ]
        for step in range(steps)
    ]
    whole_k = loads.make(k_mem, k_hbm)
    for load in small + blocks[0] + [whole_k] + blocks[1] + last:
        loads.start(load)
    for load in small:
        loads.wait(load)
    own_mark = mark_of(marks.at[0])
    bias = bias_row([jnp.where(mark_of(marks.at[d]) == own_mark, 0.0, NEG) for d in range(WIN)], rows)
    scale = 1.0 / math.sqrt(HSIZE)
    u_sum = jnp.zeros((rows, HSIZE), F32)
    copies = []
    for step in range(steps):
        for load in blocks[step] + ([whole_k] if step == 0 else []):
            loads.wait(load)
        if step + 2 < steps:
            for load in blocks[step + 2]:
                loads.start(load)
        base = step * 2 * span
        for j in range(PER):
            head = step * PER + j
            top = slice(base + j * rows, base + (j + 1) * rows)
            low = slice(base + span + j * rows, base + span + (j + 1) * rows)
            cols = head_cols(head)
            queries = jnp.concatenate([later[d, top, :] for d in range(WIN)], axis=0)
            d_outs = jnp.concatenate([later[d, low, :] for d in range(WIN)], axis=0)
            log_total = jnp.concatenate([stats[d, head : head + 1, :] for d in range(WIN)], axis=1)
            delta = jnp.concatenate([stats[d, heads + head : heads + head + 1, :] for d in range(WIN)], axis=1)
            probs = jnp.exp2(dot_nt(own[top, :], queries) * factor + (bias - log_total))
            dscores = probs * (dot_nt(own[low, :], d_outs) - delta)
            dv_mem[:, cols] = dot_nn(probs.astype(BF16), d_outs).astype(BF16)
            tilted = dot_nn(dscores.astype(BF16), queries) * (scale * gain[head : head + 1, :])
            tilt[:, cols] = tilted
            u_sum = u_sum + k_mem[:, cols].astype(F32) * tilted
        some = pl.ds(step * PER * HSIZE, PER * HSIZE)
        copies.append(pltpu.make_async_copy(dv_mem.at[:, some], dv_hbm.at[:, some], out_sems.at[steps + step]))
        copies[-1].start()
    loads.wait(last[0])
    rk = scales[...]
    low_part = rk * rk * rk * jnp.sum(u_sum, axis=-1, keepdims=True) * (1.0 / width)
    close_norm(heads, rk, low_part, tilt, k_mem, dk_mem, dk_hbm, out_sems)
    for copy in copies:
        copy.wait()


def spread_kernel(part_ref, one_ref, two_ref, three_ref, out_ref):
    del one_ref, two_ref, three_ref
    out_ref[...] = jnp.broadcast_to(jnp.sum(part_ref[...].astype(F32), axis=0).astype(BF16)[None], out_ref.shape)


def gains_kernel(part_ref, gq_ref, gk_ref, dq_ref, dk_ref):
    total = jnp.sum(part_ref[...].astype(F32), axis=0)
    dq_ref[...] = total
    dk_ref[...] = total * gq_ref[...] / gk_ref[...]


def params(limit=VMEM_LIMIT):
    return pltpu.CompilerParams(vmem_limit_bytes=limit)


def cost(flops, data=2**20):
    return pl.CostEstimate(flops=flops, bytes_accessed=data, transcendentals=0)


def shape(*dims, dtype=F32):
    return jax.ShapeDtypeStruct(dims, dtype)


def still(*dims):
    return pl.BlockSpec(dims, lambda i, odd: (0,) * len(dims))


def head_blocks(rows, used_if=None):
    def place(i, odd):
        if used_if is None:
            return (i, 0)
        return (i * odd[0] if used_if else i * (1 - odd[0]), 0)

    return pl.BlockSpec((PER * rows, HSIZE), place)


def body(q_in, k_in, v_in, gain_q, gain_k, d_out, video):
    rows, width = q_in.shape
    heads = width // HSIZE
    steps = heads // PER
    factor = math.log2(math.e) / math.sqrt(HSIZE)
    near_by, along = lax.axis_size("dp") * CORES, lax.axis_size("z")
    groups = near_by * along
    odd = lax.axis_index("core").astype(jnp.int32).reshape(1)
    gq = gain_q.reshape(heads, HSIZE)
    gk = gain_k.reshape(heads, HSIZE)
    packed_rows = 2 * heads * rows + MARK_ROWS
    pair_flops = 2 * rows * rows * HSIZE * heads
    smem = pl.BlockSpec(memory_space=pltpu.SMEM)
    vmem = pl.BlockSpec(memory_space=pltpu.VMEM)
    hbm = pl.BlockSpec(memory_space=pl.ANY)

    def after(value, flops, *others):
        return pl.pallas_call(
            gate_kernel,
            out_shape=jax.ShapeDtypeStruct(value.shape, value.dtype),
            in_specs=[hbm] * (1 + len(others)),
            out_specs=hbm,
            input_output_aliases={0: 0},
            compiler_params=params(),
            cost_estimate=cost(flops),
            name="gate",
        )(value, *others)

    def gridded(kernel, name, flops, in_specs, out_specs, out_shape, scratch=(), limit=VMEM_LIMIT):
        return pl.pallas_call(
            kernel,
            grid_spec=pltpu.PrefetchScalarGridSpec(
                num_scalar_prefetch=1, grid=(steps,), in_specs=in_specs, out_specs=out_specs, scratch_shapes=scratch
            ),
            out_shape=out_shape,
            compiler_params=params(limit),
            cost_estimate=cost(flops),
            name=name,
        )

    packed = shape(packed_rows, HSIZE, dtype=BF16)
    a, b, rq, rk = pl.pallas_call(
        functools.partial(pack_kernel, heads),
        out_shape=(packed, packed, shape(rows, HSIZE), shape(rows, HSIZE)),
        in_specs=[smem, smem] + [hbm] * 6,
        out_specs=(hbm,) * 4,
        scratch_shapes=[
            pltpu.VMEM((4, rows, width), BF16),
            pltpu.VMEM((4, heads * rows, HSIZE), BF16),
            pltpu.VMEM((2, heads, HSIZE), F32),
            pltpu.VMEM((MARK_ROWS, HSIZE), BF16),
            pltpu.VMEM((2, rows, HSIZE), F32),
            pltpu.SemaphoreType.DMA((4, SPLIT + 1)),
            pltpu.SemaphoreType.DMA((4, steps + 1)),
        ],
        compiler_params=params(),
        cost_estimate=cost(pair_flops),
        name="pack",
    )(odd, video, q_in, k_in, d_out, v_in, gq, gk)

    cross = [(i, i + 1) for i in range(1, groups - 1, 2)] + [(i, i - 1) for i in range(2, groups, 2)]
    chip = [(i, i ^ 1) for i in range(groups)]
    next_chip = [(i, i + 2) for i in range(0, groups - 2, 2)] + [(i, i - 2) for i in range(3, groups, 2)]
    both = head_blocks(2 * rows)
    if_odd = head_blocks(2 * rows, True)
    if_even = head_blocks(2 * rows, False)
    tall = head_blocks(rows)
    mark = pl.BlockSpec((MARK_ROWS, HSIZE), lambda i, odd: (2 * heads * rows // MARK_ROWS, 0))
    cols = pl.BlockSpec((rows, PER * HSIZE), lambda i, odd: (0, i))
    square = still(rows, HSIZE)
    whole = still(rows, width)
    sums_shape = (shape(heads * rows, HSIZE),) * 3
    x1 = after(lax.ppermute(a, AXES, cross), 2 * pair_flops)
    sums = gridded(
        functools.partial(own_kernel, rows, factor), "own", 1024, [both, both], (tall,) * 3, sums_shape
    )(odd, a, b)
    b = after(b, 0, sums[2])
    x2 = lax.ppermute(b, AXES, next_chip)
    x3 = after(lax.ppermute(x1, AXES, next_chip), pair_flops)
    s1 = lax.ppermute(b, AXES, chip)
    s2 = lax.ppermute(x1, AXES, chip)
    s3 = lax.ppermute(x2, AXES, chip)

    near = gridded(
        functools.partial(near_kernel, rows, factor), "near", 1024,
        [if_even, if_odd, if_even, if_odd] + [mark] * 3 + [tall] * 3,
        (tall,) * 3,
        sums_shape,
    )(odd, a, b, x1, s1, a, x1, s1, *sums)
    block = pltpu.VMEM((2 * heads * rows, HSIZE), BF16)
    flat = pltpu.VMEM((rows, width), BF16)
    wide = pltpu.VMEM((rows, width), F32)
    marks = lambda count: pltpu.VMEM((count, MARK_ROWS, HSIZE), BF16)
    gain_mem, scale_mem = pltpu.VMEM((heads, HSIZE), F32), pltpu.VMEM((rows, HSIZE), F32)
    sum_mem = pltpu.VMEM((heads * rows, HSIZE), F32)
    whole_shape = shape(rows, width, dtype=BF16)
    dq_in, w, stats = pl.pallas_call(
        functools.partial(query_kernel, rows, heads, factor),
        out_shape=(whole_shape, shape(along, heads, HSIZE, dtype=BF16), shape(2 * heads, rows)),
        in_specs=[smem] + [hbm] * 12,
        out_specs=(hbm,) * 3,
        scratch_shapes=[block, pltpu.VMEM((2, 2 * heads * rows, HSIZE), BF16), sum_mem, sum_mem, sum_mem, flat, gain_mem,
                        scale_mem, marks(WIN - 1), wide, flat,
                        pltpu.VMEM((along, heads, HSIZE), BF16), pltpu.VMEM((2 * heads, rows), F32),
                        pltpu.SemaphoreType.DMA((6 + 6 * steps,)), pltpu.SemaphoreType.DMA((steps + 2,))],
        compiler_params=params(),
        cost_estimate=cost(1024),
        name="query_side",
    )(odd, a, b, x2, s2, x3, s3, *near, q_in, gq, rq)

    def back(value, by):
        return lax.ppermute(value, AXES, [(i, i - by) for i in range(by, groups)])

    w = lax.all_to_all(w, "z", 0, 0)
    later = [back(stats, by) for by in range(1, WIN)]
    w = pl.pallas_call(
        spread_kernel,
        out_shape=shape(near_by, heads, HSIZE, dtype=BF16),
        in_specs=[vmem] + [hbm] * 3,
        out_specs=vmem,
        compiler_params=params(SMALL_LIMIT),
        cost_estimate=cost(2**20),
        name="spread",
    )(w, *later)
    w = lax.all_to_all(w, ("dp", "core"), 0, 0)
    dgain_q, dgain_k = pl.pallas_call(
        gains_kernel,
        out_shape=(shape(heads, HSIZE),) * 2,
        in_specs=[vmem] * 3,
        out_specs=(vmem,) * 2,
        compiler_params=params(SMALL_LIMIT),
        cost_estimate=cost(2**20),
        name="gains",
    )(w, gq, gk)

    dk_in, dv_in = pl.pallas_call(
        functools.partial(key_kernel, rows, heads, factor),
        out_shape=(whole_shape, whole_shape),
        in_specs=[smem] + [hbm] * 15,
        out_specs=(hbm, hbm),
        scratch_shapes=[block, pltpu.VMEM((WIN, 2 * heads * rows, HSIZE), BF16), pltpu.VMEM((WIN, 2 * heads, rows), F32),
                        flat, gain_mem, scale_mem, marks(WIN), wide, flat, flat,
                        pltpu.SemaphoreType.DMA((2 * WIN + 3 + (WIN + 1) * steps,)), pltpu.SemaphoreType.DMA((2 * steps,))],
        compiler_params=params(KEY_LIMIT),
        cost_estimate=cost(16 * pair_flops),
        name="key_side",
    )(odd, a, b, x1, s1, x2, s2, x3, s3, stats, *later, k_in, gk, rk)
    return dq_in, dk_in, dv_in, dgain_q.reshape(width), dgain_k.reshape(width)


def solution(mesh):
    dp, seq = mesh.devices.shape
    split = Mesh(mesh.devices.reshape(dp, seq // CORES, CORES), AXES)
    rows = P(AXES, None)
    return jax.shard_map(
        body,
        mesh=split,
        in_specs=(rows, rows, rows, P(), P(), rows, P(AXES)),
        out_specs=(rows, rows, rows, P(), P()),
        check_vma=False,
    )
```
